32 devices in a mesh: cp: 4 (over y, x), dp: 8 (over z, core).
Axes of the slice: x: 2, y: 2, z: 4, core: 2. Of those that a mesh axis runs over, the one named last changes fastest.
Arguments:
- queries: bfloat16 [8, 768, 512], P('dp', 'cp'), may hold values from -6 to 6
- key_rows: bfloat16 [8, 768, 512], P('dp', 'cp'), may hold values from -6 to 6
- value_rows: bfloat16 [8, 768, 512], P('dp', 'cp'), may hold values from -6 to 6
- stream_in: bfloat16 [8, 768, 1024], P('dp', 'cp'), may hold values from -6 to 6
- out_grad: bfloat16 [8, 768, 1024], P('dp', 'cp'), may hold values from -6 to 6
- out_weight: bfloat16 [512, 1024], P('cp'), may hold values from -0.25 to 0.25
- conv_weight: float32 [7, 1024], replicated, may hold values from -3 to 3
- lengths: int32 [8], P('dp'), may hold values from 384 to 768, as said below
- offsets: int32 [8, 2], P('dp'), may hold values from 0 to 2, as said below
Outputs:
- query_grad: bfloat16 [8, 768, 512], P('dp', 'cp')
- key_grad: bfloat16 [8, 768, 512], P('dp', 'cp')
- value_grad: bfloat16 [8, 768, 512], P('dp', 'cp')
- stream_grad: bfloat16 [8, 768, 1024], P('dp', 'cp')
- weight_grad: float32 [512, 1024], P('cp')
- conv_grad: float32 [7, 1024], replicated
The draws below stay inside these ranges and needn't reach their ends.
Inputs may be any that keep to these rules, and one draw needn't show every extreme that they name: `lengths`: each a multiple of 24; some utterance has exactly 768 frames. `offsets`: column 0 is the number of earlier blocks that a block attends, at most 2; column 1 the number of later blocks, at most 1; some utterance has 2 and 1.
All inputs are finite; a program needn't handle non-finite values.
Results may differ from the reference program's by a relative error of at most 0.0069.
Values may be sent and summed in bfloat16 or wider, within the bound.
No kernel may reach another device: no remote copies, remote signals or barrier semaphores. Data moves between devices by JAX's collectives and lax.ppermute only.
A program may use at most 64 MiB of HBM per device.

```python
import jax
import jax.numpy as jnp
from jax import lax

D = 1024
HEADS = 8
HSZ = 64
BLK = 24
KW = 7
HD = 512
T_SIZE = 768
UTTS = 8


def base_field(key, salt):
    return jnp.clip(jax.random.normal(jax.random.fold_in(key, salt), (UTTS, T_SIZE, HD), jnp.float32), -5.0, 5.0)


def draw_queries(key, part):
    field = base_field(key, 11)
    return field.astype(jnp.bfloat16)


def draw_key_rows(key, part):
    field = base_field(key, 21)
    return field.astype(jnp.bfloat16)


def draw_lengths(key, part):
    block_count = T_SIZE // BLK
    counts = jax.random.randint(jax.random.fold_in(key, 3), (UTTS,), block_count // 2, block_count + 1)
    full_at = jax.random.randint(jax.random.fold_in(key, 4), (), 0, UTTS)
    counts = jnp.where(jnp.arange(UTTS) == full_at, block_count, counts)
    return (counts * BLK).astype(jnp.int32)


def draw_offsets(key, part):
    before = jax.random.randint(jax.random.fold_in(key, 5), (UTTS,), 0, 3)
    after = jax.random.randint(jax.random.fold_in(key, 6), (UTTS,), 0, 2)
    widest = jax.random.randint(jax.random.fold_in(key, 9), (), 0, UTTS)
    chosen = jnp.arange(UTTS) == widest
    before = jnp.where(chosen, 2, before)
    after = jnp.where(chosen, 1, after)
    return jnp.stack([before, after], 1).astype(jnp.int32)


def level_of(key, shape, shards, low, top_value):
    loudness = 1.0
    for position, shards_of in shards:
        steps = jax.random.uniform(jax.random.fold_in(jax.random.fold_in(key, 6), position), (shards_of,), jnp.float32, low / len(shards), top_value / len(shards))
        loudness = loudness * jnp.repeat(jnp.exp(steps), shape[position] // shards_of).reshape((-1,) + (1,) * (len(shape) - 1 - position))
    return loudness


def bell_draw(key, shape, deviation, limit, cuts=(), kind=jnp.bfloat16):
    values = deviation * jax.random.normal(key, shape, jnp.float32)
    if cuts:
        values = values * level_of(key, shape, cuts, -0.22, 0.18)
    return jnp.clip(values, -limit, limit).astype(kind)


def setup_inputs(seed: int = 0) -> dict:
    arg_keys = jax.random.split(jax.random.key(seed), 10)
    queries = draw_queries(jax.random.fold_in(arg_keys[9], 71), 0)
    key_rows = draw_key_rows(jax.random.fold_in(arg_keys[9], 71), 0)
    value_rows = bell_draw(arg_keys[2], (UTTS, T_SIZE, HD), 1.0, 6.0, ((0, 8), (1, 4)))
    stream_in = bell_draw(arg_keys[3], (UTTS, T_SIZE, D), 1.0, 6.0, ((0, 8), (1, 4)))
    out_grad = bell_draw(arg_keys[4], (UTTS, T_SIZE, D), 1.0, 6.0, ((0, 8), (1, 4)))
    out_weight = bell_draw(arg_keys[5], (HD, D), HD ** -0.5, 0.25, ((0, 4),))
    conv_weight = bell_draw(arg_keys[6], (KW, D), 0.4, 3.0, (), jnp.float32)
    lengths = draw_lengths(jax.random.fold_in(arg_keys[9], 71), 0)
    offsets = draw_offsets(jax.random.fold_in(arg_keys[9], 71), 0)
    return dict(queries=queries, key_rows=key_rows, value_rows=value_rows, stream_in=stream_in, out_grad=out_grad, out_weight=out_weight, conv_weight=conv_weight, lengths=lengths, offsets=offsets)


neg_big = -1e30


def rounded(values):
    return lax.optimization_barrier(values.astype(jnp.bfloat16)).astype(jnp.float32)


def one_utterance(query_rows, key_local, value_local, stream_rows, grad_rows, length, offset_pair, out_weight, conv_weight):
    score_scale = HSZ ** -0.5
    block_count = T_SIZE // BLK
    window_len = 4 * BLK
    half_width = KW // 2
    frames = jnp.arange(T_SIZE, dtype=jnp.int32)
    valid_rows = (frames < length).astype(jnp.float32)

    def windows_of(array):
        padded = jnp.pad(array, ((2 * BLK, BLK), (0, 0)))
        slabs = [padded[shift_at * BLK: shift_at * BLK + T_SIZE].reshape(block_count, BLK, -1) for shift_at in range(4)]
        return jnp.stack(slabs, 1).reshape(block_count, window_len, HEADS, HSZ)

    key_win = windows_of(key_local).astype(jnp.float32)
    value_win = windows_of(value_local).astype(jnp.float32)
    query_blk = query_rows.astype(jnp.float32).reshape(block_count, BLK, HEADS, HSZ)
    within = jnp.arange(window_len, dtype=jnp.int32)
    key_frames = jnp.arange(block_count, dtype=jnp.int32)[:, None] * BLK + within[None, :] - 2 * BLK
    relative = within // BLK - 2
    in_reach = (relative >= -offset_pair[0]) & (relative <= offset_pair[1])
    allowed = in_reach[None, :] & (key_frames >= 0) & (key_frames < length)
    scores = jnp.einsum('nqhd,nkhd->nhqk', query_blk, key_win) * score_scale
    masked = jnp.where(allowed[:, None, None, :], scores, neg_big)
    top_score = jnp.max(masked, axis=3, keepdims=True)
    exp_terms = jnp.exp(masked - top_score)
    softmax_w = exp_terms / jnp.sum(exp_terms, axis=3, keepdims=True)
    weight_b = rounded(softmax_w)
    attended = jnp.einsum('nhqk,nkhd->nqhd', weight_b, value_win).reshape(T_SIZE, HD)
    attended = (attended * valid_rows[:, None]).astype(jnp.bfloat16)
    projected = jnp.dot(attended, out_weight, preferred_element_type=jnp.float32)
    mixed_rows = (stream_rows.astype(jnp.float32) + projected) * valid_rows[:, None]
    grad_masked = grad_rows * valid_rows[:, None].astype(grad_rows.dtype)
    grad_pad = jnp.pad(grad_masked.astype(jnp.float32), ((half_width, half_width), (0, 0)))
    conv_sum = jnp.zeros((T_SIZE, D), jnp.float32)
    conv_terms = []
    for tap in range(KW):
        shifted = grad_pad[2 * half_width - tap: 2 * half_width - tap + T_SIZE]
        conv_sum = conv_sum + conv_weight[tap][None, :] * shifted
        conv_terms.append(jnp.sum(mixed_rows * shifted, axis=0))
    conv_local = jnp.stack(conv_terms, 0)
    stream_grad = (conv_sum * valid_rows[:, None]).astype(jnp.bfloat16)
    weight_term = jnp.dot(attended.T, stream_grad, preferred_element_type=jnp.float32)
    attn_grad = jnp.dot(stream_grad, out_weight.T, preferred_element_type=jnp.float32).astype(jnp.bfloat16)
    grad_blk = attn_grad.astype(jnp.float32).reshape(block_count, BLK, HEADS, HSZ)
    dprob = jnp.einsum('nqhd,nkhd->nhqk', grad_blk, value_win)
    inner = jnp.sum(softmax_w * dprob, axis=3, keepdims=True)
    dscore = rounded(softmax_w * (dprob - inner))
    query_grad = (jnp.einsum('nhqk,nkhd->nqhd', dscore, key_win) * score_scale).reshape(T_SIZE, HD).astype(jnp.bfloat16)
    key_win_grad = jnp.einsum('nhqk,nqhd->nkhd', dscore, query_blk) * score_scale
    value_win_grad = jnp.einsum('nhqk,nqhd->nkhd', weight_b, grad_blk)

    def fold_back(window_grad):
        parts = window_grad.reshape(block_count, 4, BLK, HD)
        total = jnp.zeros((block_count + 3, BLK, HD), jnp.float32)
        for shift_at in range(4):
            total = total + jnp.pad(parts[:, shift_at], ((shift_at, 3 - shift_at), (0, 0), (0, 0)))
        return total[2:block_count + 2].reshape(T_SIZE, HD).astype(jnp.bfloat16)

    return query_grad, fold_back(key_win_grad), fold_back(value_win_grad), stream_grad, weight_term, conv_local


def reference(queries, key_rows, value_rows, stream_in, out_grad, out_weight, conv_weight, lengths, offsets):
    def scan_step(running, per_utt):
        results = one_utterance(*per_utt, out_weight, conv_weight)
        return (running[0] + results[4], running[1] + results[5]), results[:4]

    start_acc = (jnp.zeros((HD, D), jnp.float32), jnp.zeros((KW, D), jnp.float32))
    sums, grads = lax.scan(scan_step, start_acc, (queries, key_rows, value_rows, stream_in, out_grad, lengths, offsets))
    return grads[0], grads[1], grads[2], grads[3], sums[0], sums[1]
```

```python
import functools

import jax
import jax.numpy as jnp
from jax import lax
from jax.experimental import pallas as pl
from jax.experimental.pallas import tpu as pltpu
from jax.sharding import PartitionSpec as P

HEADS = 8
HSZ = 64
BLK = 24
KW = 7
HALF = KW // 2
BACK = 2 * BLK
AHEAD = 32
EDGE = 16
TILE = 4 * BLK
REACH = 176
GROUP = 4
FEATS = GROUP * HSZ
LANES = GROUP * TILE
NEG = -1e30
BF = jnp.bfloat16
F32 = jnp.float32
VMEM = pl.BlockSpec(memory_space=pltpu.VMEM)
SMEM = pl.BlockSpec(memory_space=pltpu.SMEM)
ANY = pl.BlockSpec(memory_space=pl.ANY)


def nt(a, b):
    return lax.dot_general(a, b, (((1,), (1,)), ((), ())), preferred_element_type=F32)


def nn(a, b):
    return lax.dot_general(a, b, (((1,), (0,)), ((), ())), preferred_element_type=F32)


def tn(a, b):
    return lax.dot_general(a, b, (((0,), (0,)), ((), ())), preferred_element_type=F32)


def call(kernel, outs, ins, args, scratch=(), flops=0, moved=0):
    return pl.pallas_call(
        kernel,
        out_shape=outs,
        in_specs=ins,
        out_specs=jax.tree.map(lambda _: VMEM, outs),
        scratch_shapes=scratch,
        compiler_params=pltpu.CompilerParams(vmem_limit_bytes=40 * 1024 * 1024),
        cost_estimate=pl.CostEstimate(flops=flops, bytes_accessed=moved, transcendentals=0),
    )(*args)


def shape(dims, kind):
    return jax.ShapeDtypeStruct(dims, kind)


def pack_kernel(k, v, g, w, ahead, behind, w_half, sems):
    rows, feats = k.shape
    half = w.shape[0] // 2
    core = lax.rem(lax.axis_index("dp"), 2)
    tail = rows - BACK
    pairs = [
        (k.at[pl.ds(tail, BACK)], ahead.at[pl.ds(0, BACK)]),
        (v.at[pl.ds(tail, BACK)], ahead.at[pl.ds(BACK, BACK)]),
        (k.at[pl.ds(0, AHEAD)], behind.at[pl.ds(0, AHEAD)]),
        (v.at[pl.ds(0, AHEAD)], behind.at[pl.ds(AHEAD, AHEAD)]),
        (w.at[pl.ds(pl.multiple_of(core * half, half), half)], w_half),
    ]
    for part in range(2):
        cols = pl.ds(part * feats, feats)
        at = part * EDGE
        pairs.append((g.at[pl.ds(rows - EDGE, EDGE), cols], ahead.at[pl.ds(2 * BACK + at, EDGE)]))
        pairs.append((g.at[pl.ds(0, EDGE), cols], behind.at[pl.ds(2 * AHEAD + at, EDGE)]))
    copies = [pltpu.make_async_copy(a, b, sems.at[i]) for i, (a, b) in enumerate(pairs)]
    for copy in copies:
        copy.start()
    for copy in copies:
        copy.wait()


def packed(k, v, g, w):
    feats = k.shape[1]
    outs = (
        shape((2 * BACK + 2 * EDGE, feats), BF),
        shape((2 * AHEAD + 2 * EDGE, feats), BF),
        shape((w.shape[0] // 2, w.shape[1]), BF),
    )
    return pl.pallas_call(
        pack_kernel,
        out_shape=outs,
        in_specs=[ANY] * 4,
        out_specs=(ANY,) * 3,
        scratch_shapes=[pltpu.SemaphoreType.DMA((9,))],
    )(k, v, g, w)


def head_of(dims):
    return lax.broadcasted_iota(jnp.int32, dims, 1) // HSZ


def stacked(tile, amount):
    head = head_of((1, FEATS))
    return jnp.concatenate(
        [tile * jnp.where(head == h, amount, 0.0).astype(BF) for h in range(GROUP)], 0
    )


def unstacked(product):
    head = head_of((TILE, FEATS))
    out = product[:TILE]
    for h in range(1, GROUP):
        out = jnp.where(head == h, product[h * TILE : (h + 1) * TILE], out)
    return out


def fill_ext(ext, before, local, after):
    rows = local.shape[0]
    ext[0:BACK] = before
    ext[BACK : BACK + rows] = local[...]
    ext[BACK + rows : BACK + rows + AHEAD] = after


def allowed_in(tile, base, length, back, ahead):
    lane = lax.broadcasted_iota(jnp.int32, (1, LANES), 1)
    within = lane
    for h in range(1, GROUP):
        within = within - jnp.where(lane >= h * TILE, TILE, 0)
    block = jnp.zeros_like(lane)
    for b in range(1, TILE // BLK):
        block = block + jnp.where(within >= b * BLK, 1, 0)
    origin = base + tile * TILE - BACK
    low = jnp.maximum((block + 2 - back) * BLK, -origin)
    high = jnp.minimum((block + 3 + ahead) * BLK, length - origin)
    row = lax.broadcasted_iota(jnp.int32, (REACH, LANES), 0)
    return (row >= low) & (row < high)


def probabilities(key_tile, query_stack, allowed):
    scores = jnp.where(allowed, nt(key_tile, query_stack), NEG)
    terms = jnp.exp(scores - jnp.max(scores, axis=0, keepdims=True))
    return terms * (1.0 / jnp.sum(terms, axis=0, keepdims=True))


def fill_grad(gx, g, near, far, base, length):
    rows, width = g.shape
    feats = width // 2

    def masked(block, start):
        frame = start + lax.broadcasted_iota(jnp.int32, block.shape, 0)
        return jnp.where(frame < length, block.astype(F32), 0.0)

    for part in range(2):
        cols = slice(part * feats, (part + 1) * feats)
        top = 2 * BACK + part * EDGE
        low = 2 * AHEAD + part * EDGE
        gx[0:8, cols] = masked(near[top : top + EDGE].astype(F32)[8:], base - 8)
        gx[8 + rows : 16 + rows, cols] = masked(far[low : low + EDGE].astype(F32)[:8], base + rows)
    gx[8 : 8 + rows, :] = masked(g[...], base)


def forward_kernel(
    q, k, v, near, far, g, taps, lengths, offsets,
    stream_grad, send, keep, att_out, kx, vx, gx, att_t,
):
    rows, feats = q.shape
    width = g.shape[1]
    place = lax.axis_index("cp")
    core = lax.rem(lax.axis_index("dp"), 2)
    base = place * rows
    length = lengths[0]
    fill_ext(kx, near[0:BACK], k, far[0:AHEAD])
    fill_ext(vx, near[BACK : 2 * BACK], v, far[AHEAD : 2 * AHEAD])
    for tile in range(rows // TILE):
        start = tile * TILE
        allowed = allowed_in(tile, base, length, offsets[0, 0], offsets[0, 1])
        frame = base + start + lax.broadcasted_iota(jnp.int32, (TILE, FEATS), 0)
        for group in range(feats // FEATS):
            cols = slice(group * FEATS, (group + 1) * FEATS)
            query_stack = stacked(q[start : start + TILE, cols], HSZ**-0.5)
            probs = probabilities(kx[start : start + REACH, cols], query_stack, allowed)
            product = tn(probs.astype(BF), vx[start : start + REACH, cols])
            attended = jnp.where(frame < length, unstacked(product), 0.0).astype(BF)
            att_out[start : start + TILE, cols] = attended
    att_t[...] = att_out[...].astype(F32).T.astype(BF)
    fill_grad(gx, g, near, far, base, length)
    step = 128
    frame = base + lax.broadcasted_iota(jnp.int32, (rows, step), 0)
    for at in range(0, width, step):
        cols = slice(at, at + step)
        total = taps[0:1, cols] * gx[8 + HALF : 8 + HALF + rows, cols]
        for tap in range(1, KW):
            top = 8 + HALF - tap
            total = total + taps[tap : tap + 1, cols] * gx[top : top + rows, cols]
        stream_grad[:, cols] = jnp.where(frame < length, total, 0.0).astype(BF)
    half = send.shape[1]
    for part in range(send.shape[0]):
        there = pl.multiple_of(2 * half * part + half * (1 - core), half)
        here = pl.multiple_of(2 * half * part + half * core, half)
        send[part] = nn(att_t[pl.ds(there, half)], stream_grad[...]).astype(BF)
        keep[part] = nn(att_t[pl.ds(here, half)], stream_grad[...])


def split_kernel(parts, keep, got, own, *pieces):
    place = lax.axis_index("cp")
    own[...] = keep[place] + got[place].astype(F32)
    for k, piece in enumerate(pieces, 1):
        at = lax.bitwise_xor(place, k)
        piece[...] = (keep[at] + got[at].astype(F32)).astype(BF)


def tree_sum(terms):
    while len(terms) > 1:
        terms = [a + b for a, b in zip(terms[::2], terms[1::2])]
    return terms[0]


def rescatter_kernel(count, own, *refs):
    got, outs = refs[: count - 1], refs[count - 1 :]
    total = own[...]
    for ref in got:
        total = total + ref[...].astype(F32)
    (mine, *pieces), hold = outs[:-1], outs[-1]
    hold[...] = total
    chunk = mine.shape[0]
    floor = lax.div(lax.axis_index("dp"), 2)
    mine[...] = hold[pl.ds(pl.multiple_of(floor * chunk, chunk), chunk)]
    for k, piece in enumerate(pieces, 1):
        at = lax.bitwise_xor(floor, k)
        piece[...] = hold[pl.ds(pl.multiple_of(at * chunk, chunk), chunk)].astype(BF)


def chunk_kernel(count, own, *refs):
    total = own[...]
    for ref in refs[: count - 1]:
        total = total + ref[...].astype(F32)
    refs[-1][...] = total.astype(BF)


def final_kernel(count, *refs):
    mine, theirs = refs[:count], refs[count : 2 * count]
    conv_here, conv_there, weight_grad, conv_grad = refs[2 * count :]
    chunk = mine[0].shape[0]
    half = chunk * count
    core = lax.rem(lax.axis_index("dp"), 2)
    floor = lax.div(lax.axis_index("dp"), 2)
    for side, group in ((core, mine), (1 - core, theirs)):
        for k, ref in enumerate(group):
            at = side * half + lax.bitwise_xor(floor, k) * chunk
            weight_grad[pl.ds(pl.multiple_of(at, chunk), chunk)] = ref[...].astype(F32)
    conv_grad[...] = (conv_here[...] + conv_there[...])[:KW]


def backward_kernel(
    count, q, k, v, near, far, g, stream, stream_grad, att, w, lengths, offsets, *refs
):
    got = refs[: count - 1]
    passed = refs[count - 1 : 2 * count - 2]
    query_g, key_g, value_g, key_up, key_down, conv, kx, vx, gx, wx, kg, vg, mixed, ag = refs[2 * count - 2 :]
    rows, feats = q.shape
    width = g.shape[1]
    place = lax.axis_index("cp")
    core = lax.rem(lax.axis_index("dp"), 2)
    base = place * rows
    length = lengths[0]
    shard = w.shape[0]
    half = shard // 2
    wx[pl.ds(pl.multiple_of(place * shard, shard), shard)] = w[...]
    for k_at, (a, b) in enumerate(zip(got, passed), 1):
        at = lax.bitwise_xor(place, k_at) * shard
        wx[pl.ds(pl.multiple_of(at + core * half, half), half)] = a[...]
        wx[pl.ds(pl.multiple_of(at + (1 - core) * half, half), half)] = b[...]
    ag[...] = nt(stream_grad[...], wx[...]).astype(BF)
    fill_ext(kx, near[0:BACK], k, far[0:AHEAD])
    fill_ext(vx, near[BACK : 2 * BACK], v, far[AHEAD : 2 * AHEAD])
    kg[...] = jnp.zeros_like(kg)
    vg[...] = jnp.zeros_like(vg)
    for tile in range(rows // TILE):
        start = tile * TILE
        allowed = allowed_in(tile, base, length, offsets[0, 0], offsets[0, 1])
        span = slice(start, start + REACH)
        for group in range(feats // FEATS):
            cols = slice(group * FEATS, (group + 1) * FEATS)
            query_stack = stacked(q[start : start + TILE, cols], HSZ**-0.5)
            grad_stack = stacked(ag[start : start + TILE, cols], 1.0)
            probs = probabilities(kx[span, cols], query_stack, allowed)
            dprob = nt(vx[span, cols], grad_stack)
            inner = jnp.sum(probs * dprob, axis=0, keepdims=True)
            dscore = (probs * (dprob - inner)).astype(BF)
            query_g[start : start + TILE, cols] = (
                unstacked(tn(dscore, kx[span, cols])) * HSZ**-0.5
            ).astype(BF)
            kg[span, cols] += nn(dscore, query_stack)
            vg[span, cols] += nn(probs.astype(BF), grad_stack)
    key_g[...] = kg[BACK : BACK + rows]
    value_g[...] = vg[BACK : BACK + rows]
    key_up[0:BACK] = kg[0:BACK].astype(BF)
    key_up[BACK : 2 * BACK] = vg[0:BACK].astype(BF)
    key_down[0:AHEAD] = kg[BACK + rows : BACK + rows + AHEAD].astype(BF)
    key_down[AHEAD : 2 * AHEAD] = vg[BACK + rows : BACK + rows + AHEAD].astype(BF)
    fill_grad(gx, g, near, far, base, length)
    step = 128
    frame = base + lax.broadcasted_iota(jnp.int32, (rows, width), 0)
    total = stream[...].astype(F32) + nn(att[...], wx[...])
    mixed[...] = jnp.where(frame < length, total, 0.0)
    conv[KW:] = jnp.zeros((8 - KW, width), F32)
    for at in range(0, width, step):
        cols = slice(at, at + step)
        block = mixed[:, cols]
        for tap in range(KW):
            top = 8 + HALF - tap
            conv[tap : tap + 1, cols] = jnp.sum(
                block * gx[top : top + rows, cols], axis=0, keepdims=True
            )


def join_kernel(key_g, value_g, up, down, key_out, value_out):
    rows = key_g.shape[0]
    for at, grad, out in ((0, key_g, key_out), (1, value_g, value_out)):
        first = down[at * AHEAD : (at + 1) * AHEAD].astype(F32)
        last = up[at * BACK : (at + 1) * BACK].astype(F32)
        out[0:AHEAD] = (grad[0:AHEAD] + first).astype(BF)
        out[AHEAD : rows - BACK] = grad[AHEAD : rows - BACK].astype(BF)
        out[rows - BACK :] = (grad[rows - BACK :] + last).astype(BF)


def conv_sum_kernel(*refs):
    refs[-1][...] = tree_sum([ref[...] for ref in refs[:-1]])


def body(
    queries, key_rows, value_rows, stream_in, out_grad, out_weight, conv_weight, lengths, offsets
):
    rows, feats = queries.shape[1:]
    width = stream_in.shape[2]
    cps, dps = lax.axis_size("cp"), lax.axis_size("dp")
    floors = dps // 2
    q, k, v, g, stream = queries[0], key_rows[0], value_rows[0], out_grad[0], stream_in[0]
    shard = out_weight.shape[0]
    half = shard // 2
    up = [(i, i + 1) for i in range(cps - 1)]
    down = [(i + 1, i) for i in range(cps - 1)]
    other_core = [(i, i ^ 1) for i in range(dps)]

    def over_cp(array, by):
        return lax.ppermute(array, "cp", [(i, i ^ by) for i in range(cps)])

    def over_z(array, by):
        return lax.ppermute(array, "dp", [(i, i ^ (2 * by)) for i in range(dps)])

    def over_core(array):
        return lax.ppermute(array, "dp", other_core)

    ahead, behind, w_half = packed(k, v, g, out_weight)
    near = lax.ppermute(ahead, "cp", up)
    far = lax.ppermute(behind, "cp", down)
    w_got = [over_cp(w_half, by) for by in range(1, cps)]
    ext = rows + BACK + AHEAD
    stream_grad, send, keep, att = call(
        forward_kernel,
        (
            shape((rows, width), BF),
            shape((cps, half, width), BF),
            shape((cps, half, width), F32),
            shape((rows, feats), BF),
        ),
        [VMEM] * 7 + [SMEM] * 2,
        (q, k, v, near, far, g, conv_weight, lengths, offsets),
        [
            pltpu.VMEM((ext, feats), BF),
            pltpu.VMEM((ext, feats), BF),
            pltpu.VMEM((rows + 16, width), F32),
            pltpu.VMEM((feats, rows), BF),
        ],
        flops=2 * rows * feats * width,
        moved=6 * 2**20,
    )
    w_passed = [over_core(part) for part in w_got]
    core_got = over_core(send)
    own, *pieces = call(
        functools.partial(split_kernel, cps),
        (shape((half, width), F32),) + (shape((half, width), BF),) * (cps - 1),
        [VMEM] * 2,
        (keep, core_got),
        moved=3 * 2**20,
    )
    cp_got = [over_cp(piece, by) for by, piece in enumerate(pieces, 1)]
    query_g, key_g, value_g, key_up, key_down, conv = call(
        functools.partial(backward_kernel, cps),
        (
            shape((rows, feats), BF),
            shape((rows, feats), F32),
            shape((rows, feats), F32),
            shape((2 * BACK, feats), BF),
            shape((2 * AHEAD, feats), BF),
            shape((8, width), F32),
        ),
        [VMEM] * 10 + [SMEM] * 2 + [VMEM] * (2 * cps - 2),
        (q, k, v, near, far, g, stream, stream_grad, att, out_weight, lengths, offsets)
        + tuple(w_got)
        + tuple(w_passed),
        [
            pltpu.VMEM((ext, feats), BF),
            pltpu.VMEM((ext, feats), BF),
            pltpu.VMEM((rows + 16, width), F32),
            pltpu.VMEM((feats, width), BF),
            pltpu.VMEM((ext, feats), F32),
            pltpu.VMEM((ext, feats), F32),
            pltpu.VMEM((rows, width), F32),
            pltpu.VMEM((rows, feats), BF),
        ],
        flops=4 * rows * feats * width,
        moved=8 * 2**20,
    )
    from_up = lax.ppermute(key_up, "cp", down)
    from_down = lax.ppermute(key_down, "cp", up)
    conv_cp = call(
        conv_sum_kernel,
        shape((8, width), F32),
        [VMEM] * cps,
        (conv, *[over_cp(conv, by) for by in range(1, cps)]),
    )
    if floors != 4 or half % (16 * floors):
        summed = own
        for got in cp_got:
            summed = summed + got.astype(F32)
        at = (lax.axis_index("dp") % 2) * half
        whole = lax.dynamic_update_slice(jnp.zeros((shard, width), F32), summed, (at, 0))
        weight_grad = lax.psum(whole, "dp")
        conv_grad = lax.psum(conv_cp, "dp")[:KW]
    else:
        chunk = half // floors
        mine, *z_pieces = call(
            lambda *refs: rescatter_kernel(cps, *refs),
            (shape((chunk, width), F32),) + (shape((chunk, width), BF),) * (floors - 1),
            [VMEM] * cps,
            (own, *cp_got),
            [pltpu.VMEM((half, width), F32)],
            moved=2**20,
        )
        z_got = [over_z(piece, by) for by, piece in enumerate(z_pieces, 1)]
        conv_z = call(
            conv_sum_kernel,
            shape((8, width), F32),
            [VMEM] * floors,
            (conv_cp, *[over_z(conv_cp, by) for by in range(1, floors)]),
        )
        final = call(
            lambda *refs: chunk_kernel(floors, *refs),
            shape((chunk, width), BF),
            [VMEM] * floors,
            (mine, *z_got),
        )
        here = [final] + [over_z(final, by) for by in range(1, floors)]
        there = [over_core(part) for part in here]
        weight_grad, conv_grad = call(
            lambda *refs: final_kernel(floors, *refs),
            (shape((shard, width), F32), shape((KW, width), F32)),
            [VMEM] * (2 * floors + 2),
            (*here, *there, conv_z, over_core(conv_z)),
        )
    key_grad, value_grad = call(
        join_kernel,
        (shape((rows, feats), BF),) * 2,
        [VMEM] * 4,
        (key_g, value_g, from_up, from_down),
        moved=2**20,
    )
    return (
        query_g[None],
        key_grad[None],
        value_grad[None],
        stream_grad[None],
        weight_grad,
        conv_grad,
    )


def solution(mesh):
    rows_spec = P("dp", "cp", None)
    return jax.shard_map(
        body,
        mesh=mesh,
        in_specs=(rows_spec,) * 5 + (P("cp", None), P(), P("dp"), P("dp", None)),
        out_specs=(rows_spec,) * 4 + (P("cp", None), P()),
        check_vma=False,
    )
```

```python
import functools

import jax
import jax.numpy as jnp
from jax import lax
from jax.experimental import pallas as pl
from jax.experimental.pallas import tpu as pltpu
from jax.sharding import PartitionSpec as P

HEADS = 8
HSZ = 64
BLK = 24
KW = 7
HALF = KW // 2
BACK = 2 * BLK
AHEAD = 32
EDGE = 16
TILE = 4 * BLK
REACH = 176
GROUP = 4
FEATS = GROUP * HSZ
LANES = GROUP * TILE
NEG = -1e30
BF = jnp.bfloat16
F32 = jnp.float32
VMEM = pl.BlockSpec(memory_space=pltpu.VMEM)
SMEM = pl.BlockSpec(memory_space=pltpu.SMEM)
ANY = pl.BlockSpec(memory_space=pl.ANY)


def nt(a, b):
    return lax.dot_general(a, b, (((1,), (1,)), ((), ())), preferred_element_type=F32)


def nn(a, b):
    return lax.dot_general(a, b, (((1,), (0,)), ((), ())), preferred_element_type=F32)


def tn(a, b):
    return lax.dot_general(a, b, (((0,), (0,)), ((), ())), preferred_element_type=F32)


def call(kernel, outs, ins, args, scratch=(), flops=0, moved=0):
    return pl.pallas_call(
        kernel,
        out_shape=outs,
        in_specs=ins,
        out_specs=jax.tree.map(lambda _: VMEM, outs),
        scratch_shapes=scratch,
        compiler_params=pltpu.CompilerParams(vmem_limit_bytes=40 * 1024 * 1024),
        cost_estimate=pl.CostEstimate(flops=flops, bytes_accessed=moved, transcendentals=0),
    )(*args)


def shape(dims, kind):
    return jax.ShapeDtypeStruct(dims, kind)


def pack_kernel(k, v, g, w, ahead, behind, w_half, edge, sems):
    rows = k.shape[0]
    feats = k.shape[1]
    half = w.shape[0] // 2
    core = lax.rem(lax.axis_index("dp"), 2)
    pairs = [
        (k.at[pl.ds(rows - BACK, BACK)], ahead.at[pl.ds(0, BACK)]),
        (v.at[pl.ds(rows - BACK, BACK)], ahead.at[pl.ds(BACK, BACK)]),
        (k.at[pl.ds(0, AHEAD)], behind.at[pl.ds(0, AHEAD)]),
        (v.at[pl.ds(0, AHEAD)], behind.at[pl.ds(AHEAD, AHEAD)]),
        (g.at[pl.ds(rows - EDGE, EDGE)], edge.at[0]),
        (g.at[pl.ds(0, EDGE)], edge.at[1]),
        (w.at[pl.ds(pl.multiple_of(core * half, half), half)], w_half),
    ]
    copies = [pltpu.make_async_copy(a, b, sems.at[i]) for i, (a, b) in enumerate(pairs)]
    for copy in copies:
        copy.start()
    for copy in copies:
        copy.wait()
    last = edge[0].astype(F32)[8:]
    first = edge[1].astype(F32)[:8]
    for out, block in ((ahead, last), (behind, first)):
        two = jnp.concatenate([block[:, :feats], block[:, feats:]], 0)
        out[out.shape[0] - EDGE :] = two.astype(BF)


def packed(k, v, g, w):
    feats = k.shape[1]
    outs = (
        shape((2 * BACK + EDGE, feats), BF),
        shape((2 * AHEAD + EDGE, feats), BF),
        shape((w.shape[0] // 2, w.shape[1]), BF),
    )
    return pl.pallas_call(
        pack_kernel,
        out_shape=outs,
        in_specs=[ANY] * 4,
        out_specs=(VMEM,) * 3,
        scratch_shapes=[pltpu.VMEM((2, EDGE, g.shape[1]), BF), pltpu.SemaphoreType.DMA((7,))],
    )(k, v, g, w)


def head_of(dims):
    return lax.broadcasted_iota(jnp.int32, dims, 1) // HSZ


def stacked(tile, amount):
    head = head_of((1, FEATS))
    return jnp.concatenate(
        [tile * jnp.where(head == h, amount, 0.0).astype(BF) for h in range(GROUP)], 0
    )


def unstacked(product):
    head = head_of((TILE, FEATS))
    out = product[:TILE]
    for h in range(1, GROUP):
        out = jnp.where(head == h, product[h * TILE : (h + 1) * TILE], out)
    return out


def fill_ext(kx, vx, k, v, near, far):
    rows = k.shape[0]
    for at, ext, local in ((0, kx, k), (1, vx, v)):
        ext[0:BACK] = near[at * BACK : (at + 1) * BACK]
        ext[BACK : BACK + rows] = local[...]
        ext[BACK + rows :] = far[at * AHEAD : (at + 1) * AHEAD]


def allowed_in(tile, base, length, back, ahead):
    lane = lax.broadcasted_iota(jnp.int32, (1, LANES), 1)
    within = lane
    for h in range(1, GROUP):
        within = within - jnp.where(lane >= h * TILE, TILE, 0)
    block = jnp.zeros_like(lane)
    for b in range(1, TILE // BLK):
        block = block + jnp.where(within >= b * BLK, 1, 0)
    origin = base + tile * TILE - BACK
    low = jnp.maximum((block + 2 - back) * BLK, -origin)
    high = jnp.minimum((block + 3 + ahead) * BLK, length - origin)
    row = lax.broadcasted_iota(jnp.int32, (REACH, LANES), 0)
    return (row >= low) & (row < high)


def probabilities(key_tile, query_stack, allowed):
    scores = jnp.where(allowed, nt(key_tile, query_stack), NEG)
    terms = jnp.exp(scores - jnp.max(scores, axis=0, keepdims=True))
    return terms * (1.0 / jnp.sum(terms, axis=0, keepdims=True))


def masked(block, start, length):
    frame = start + lax.broadcasted_iota(jnp.int32, block.shape, 0)
    return jnp.where((frame >= 0) & (frame < length), block.astype(F32), 0.0)


def fill_rims(gx, at, near, far, base, rows, length):
    feats = near.shape[1]
    before = near[2 * BACK :].astype(F32)
    after = far[2 * AHEAD :].astype(F32)
    for part in range(2):
        cols = slice(part * feats, (part + 1) * feats)
        here = slice(part * 8, (part + 1) * 8)
        gx[0:8, cols] = masked(before[here], base - 8, length)
        gx[at : at + 8, cols] = masked(after[here], base + rows, length)


def convolve(out, out_at, gx, gx_at, taps, start, count, length):
    width = out.shape[1]
    step = 128
    frame = start + lax.broadcasted_iota(jnp.int32, (count, step), 0)
    for at in range(0, width, step):
        cols = slice(at, at + step)
        total = taps[0:1, cols] * gx[gx_at + HALF : gx_at + HALF + count, cols]
        for tap in range(1, KW):
            top = gx_at + HALF - tap
            total = total + taps[tap : tap + 1, cols] * gx[top : top + count, cols]
        out[out_at : out_at + count, cols] = jnp.where(frame < length, total, 0.0).astype(BF)


def inner_conv_kernel(g, taps, lengths, out, gx):
    rows = g.shape[0]
    base = lax.axis_index("cp") * rows
    gx[0:8] = jnp.zeros((8, gx.shape[1]), F32)
    gx[8 + rows :] = jnp.zeros((8, gx.shape[1]), F32)
    gx[8 : 8 + rows] = masked(g[...], base, lengths[0])
    convolve(out, 0, gx, 8, taps, base, rows, lengths[0])


def forward_kernel(
    q, k, v, near, far, g, taps, inner, lengths, offsets,
    stream_grad, send, keep, att_out, kx, vx, gx, att_t,
):
    rows, feats = q.shape
    place = lax.axis_index("cp")
    core = lax.rem(lax.axis_index("dp"), 2)
    base = place * rows
    length = lengths[0]
    fill_ext(kx, vx, k, v, near, far)
    for tile in range(rows // TILE):
        start = tile * TILE
        allowed = allowed_in(tile, base, length, offsets[0, 0], offsets[0, 1])
        frame = base + start + lax.broadcasted_iota(jnp.int32, (TILE, FEATS), 0)
        for group in range(feats // FEATS):
            cols = slice(group * FEATS, (group + 1) * FEATS)
            query_stack = stacked(q[start : start + TILE, cols], HSZ**-0.5)
            probs = probabilities(kx[start : start + REACH, cols], query_stack, allowed)
            product = tn(probs.astype(BF), vx[start : start + REACH, cols])
            attended = jnp.where(frame < length, unstacked(product), 0.0).astype(BF)
            att_out[start : start + TILE, cols] = attended
    att_t[...] = att_out[...].astype(F32).T.astype(BF)
    fill_rims(gx, 56, near, far, base, rows, length)
    gx[8:32] = masked(g[0:32].astype(F32)[:24], base, length)
    gx[32:56] = masked(g[rows - 32 :].astype(F32)[8:], base + rows - 24, length)
    stream_grad[EDGE : rows - EDGE] = inner[EDGE : rows - EDGE]
    convolve(stream_grad, 0, gx, 8, taps, base, EDGE, length)
    convolve(stream_grad, rows - EDGE, gx, 40, taps, base + rows - EDGE, EDGE, length)
    half = send.shape[1]
    for part in range(send.shape[0]):
        there = pl.multiple_of(2 * half * part + half * (1 - core), half)
        here = pl.multiple_of(2 * half * part + half * core, half)
        send[part] = nn(att_t[pl.ds(there, half)], stream_grad[...]).astype(BF)
        keep[part] = nn(att_t[pl.ds(here, half)], stream_grad[...])


def folded(conv, half):
    extra = 8 * conv.shape[1] // half
    return jnp.concatenate(
        [conv[:, at : at + extra] for at in range(0, conv.shape[1], extra)], 0
    )


def split_kernel(keep, got, conv, own, *pieces):
    place = lax.axis_index("cp")
    half, width = keep.shape[1:]
    tail = folded(conv[...], half).astype(BF)
    own[:, :width] = keep[place] + got[place].astype(F32)
    own[:, width:] = tail.astype(F32)
    for by, piece in enumerate(pieces, 1):
        at = lax.bitwise_xor(place, by)
        piece[:, :width] = (keep[at] + got[at].astype(F32)).astype(BF)
        piece[:, width:] = tail


def tree_sum(terms):
    while len(terms) > 1:
        terms = [a + b for a, b in zip(terms[::2], terms[1::2])]
    return terms[0]


def cp_sum_kernel(after, own, *refs):
    got = refs[:-5]
    back, onward, part, back_out, onward_out = refs[-5:]
    total = tree_sum([own[...]] + [ref[...].astype(F32) for ref in got])
    part[...] = total.astype(BF)
    back_out[...] = back[...]
    onward_out[...] = onward[...]


def z_sum_kernel(after, *refs):
    refs[-1][...] = tree_sum([ref[...].astype(F32) for ref in refs[:-1]])


def final_kernel(mine, theirs, weight_grad, conv_grad):
    half = mine.shape[0]
    width = weight_grad.shape[1]
    core = lax.rem(lax.axis_index("dp"), 2)
    weight_grad[pl.ds(pl.multiple_of(core * half, half), half)] = mine[:, :width]
    weight_grad[pl.ds(pl.multiple_of((1 - core) * half, half), half)] = theirs[:, :width]
    extra = mine.shape[1] - width
    total = mine[:, width:] + theirs[:, width:]
    for at in range(0, half, 8):
        cols = slice(at // 8 * extra, (at // 8 + 1) * extra)
        conv_grad[:, cols] = total[at : at + KW]


def weight_stack_kernel(after, *refs):
    for k, ref in enumerate(refs[:-1]):
        refs[-1][k] = ref[...]


def conv_kernel(att, w, passed, stream, g, near, far, lengths, *refs):
    got = refs[:-4]
    conv, wx, gx, mixed = refs[-4:]
    rows, width = g.shape
    place = lax.axis_index("cp")
    core = lax.rem(lax.axis_index("dp"), 2)
    base = place * rows
    length = lengths[0]
    shard = w.shape[0]
    half = shard // 2
    wx[pl.ds(pl.multiple_of(place * shard, shard), shard)] = w[...]
    for by, ref in enumerate(got, 1):
        at = lax.bitwise_xor(place, by) * shard
        wx[pl.ds(pl.multiple_of(at + core * half, half), half)] = ref[...]
        wx[pl.ds(pl.multiple_of(at + (1 - core) * half, half), half)] = passed[by - 1]
    fill_rims(gx, 8 + rows, near, far, base, rows, length)
    gx[8 : 8 + rows] = masked(g[...], base, length)
    total = stream[...].astype(F32) + nn(att[...], wx[...])
    mixed[...] = masked(total, base, length)
    conv[KW:] = jnp.zeros((8 - KW, width), F32)
    step = 128
    for at in range(0, width, step):
        cols = slice(at, at + step)
        block = mixed[:, cols]
        for tap in range(KW):
            top = 8 + HALF - tap
            conv[tap : tap + 1, cols] = jnp.sum(
                block * gx[top : top + rows, cols], axis=0, keepdims=True
            )


def backward_kernel(
    after, q, k, v, near, far, stream_grad, wx, lengths, offsets,
    query_g, key_g, value_g, back, onward, kx, vx, kg, vg, ag,
):
    rows, feats = q.shape
    base = lax.axis_index("cp") * rows
    length = lengths[0]
    ag[...] = nt(stream_grad[...], wx[...]).astype(BF)
    fill_ext(kx, vx, k, v, near, far)
    kg[...] = jnp.zeros_like(kg)
    vg[...] = jnp.zeros_like(vg)
    for tile in range(rows // TILE):
        start = tile * TILE
        allowed = allowed_in(tile, base, length, offsets[0, 0], offsets[0, 1])
        span = slice(start, start + REACH)
        for group in range(feats // FEATS):
            cols = slice(group * FEATS, (group + 1) * FEATS)
            query_stack = stacked(q[start : start + TILE, cols], HSZ**-0.5)
            grad_stack = stacked(ag[start : start + TILE, cols], 1.0)
            probs = probabilities(kx[span, cols], query_stack, allowed)
            dprob = nt(vx[span, cols], grad_stack)
            inner = jnp.sum(probs * dprob, axis=0, keepdims=True)
            dscore = (probs * (dprob - inner)).astype(BF)
            query_g[start : start + TILE, cols] = (
                unstacked(tn(dscore, kx[span, cols])) * HSZ**-0.5
            ).astype(BF)
            kg[span, cols] += nn(dscore, query_stack)
            vg[span, cols] += nn(probs.astype(BF), grad_stack)
    key_g[...] = kg[BACK : BACK + rows]
    value_g[...] = vg[BACK : BACK + rows]
    for at, ext in ((0, kg), (1, vg)):
        back[at * BACK : (at + 1) * BACK] = ext[0:BACK].astype(BF)
        onward[at * AHEAD : (at + 1) * AHEAD] = ext[BACK + rows :].astype(BF)


def join_kernel(key_g, value_g, last, first, key_out, value_out):
    rows = key_g.shape[0]
    for at, grad, out in ((0, key_g, key_out), (1, value_g, value_out)):
        out[0:AHEAD] = (
            grad[0:AHEAD] + first[at * AHEAD : (at + 1) * AHEAD].astype(F32)
        ).astype(BF)
        out[AHEAD : rows - BACK] = grad[AHEAD : rows - BACK].astype(BF)
        out[rows - BACK :] = (
            grad[rows - BACK :] + last[at * BACK : (at + 1) * BACK].astype(F32)
        ).astype(BF)


def body(
    queries, key_rows, value_rows, stream_in, out_grad, out_weight, conv_weight, lengths, offsets
):
    rows, feats = queries.shape[1:]
    width = stream_in.shape[2]
    cps, dps = lax.axis_size("cp"), lax.axis_size("dp")
    floors = dps // 2
    q, k, v, g, stream = queries[0], key_rows[0], value_rows[0], out_grad[0], stream_in[0]
    shard = out_weight.shape[0]
    half = shard // 2
    ext = rows + BACK + AHEAD
    upward = [(i, (i + 1) % cps) for i in range(cps)]
    downward = [(i, (i - 1) % cps) for i in range(cps)]

    def over_cp(arrays):
        return [
            lax.ppermute(array, "cp", [(i, i ^ by) for i in range(cps)])
            for by, array in enumerate(arrays, 1)
        ]

    def over_z(array):
        return [
            lax.ppermute(array, "dp", [(i, i ^ (2 * by)) for i in range(dps)])
            for by in range(1, floors)
        ]

    def over_core(array):
        return lax.ppermute(array, "dp", [(i, i ^ 1) for i in range(dps)])

    ahead, behind, w_half = packed(k, v, g, out_weight)
    near = lax.ppermute(ahead, "cp", upward)
    far = lax.ppermute(behind, "cp", downward)
    w_got = over_cp([w_half] * (cps - 1))
    inner = call(
        inner_conv_kernel,
        shape((rows, width), BF),
        [VMEM] * 2 + [SMEM],
        (g, conv_weight, lengths),
        [pltpu.VMEM((rows + 16, width), F32)],
    )
    ext_scratch = [pltpu.VMEM((ext, feats), BF)] * 2
    stream_grad, send, keep, att = call(
        forward_kernel,
        (
            shape((rows, width), BF),
            shape((cps, half, width), BF),
            shape((cps, half, width), F32),
            shape((rows, feats), BF),
        ),
        [VMEM] * 8 + [SMEM] * 2,
        (q, k, v, near, far, g, conv_weight, inner, lengths, offsets),
        ext_scratch + [pltpu.VMEM((64, width), F32), pltpu.VMEM((feats, rows), BF)],
    )
    core_got = over_core(send)
    passed = over_core(
        call(
            weight_stack_kernel,
            shape((cps - 1, half, width), BF),
            [ANY] + [VMEM] * (cps - 1),
            (att, *w_got),
        )
    )
    conv, wx = call(
        conv_kernel,
        (shape((8, width), F32), shape((feats, width), BF)),
        [VMEM] * 7 + [SMEM] + [VMEM] * (cps - 1),
        (att, out_weight, passed, stream, g, near, far, lengths, *w_got),
        [pltpu.VMEM((rows + 16, width), F32), pltpu.VMEM((rows, width), F32)],
    )
    wide = width + 8 * width // half
    own, *pieces = call(
        split_kernel,
        (shape((half, wide), F32),) + (shape((half, wide), BF),) * (cps - 1),
        [VMEM] * 3,
        (keep, core_got, conv),
    )
    cp_got = over_cp(pieces)
    query_g, key_g, value_g, back, onward = call(
        backward_kernel,
        (
            shape((rows, feats), BF),
            shape((rows, feats), F32),
            shape((rows, feats), F32),
            shape((2 * BACK, feats), BF),
            shape((2 * AHEAD, feats), BF),
        ),
        [ANY] + [VMEM] * 7 + [SMEM] * 2,
        (own, q, k, v, near, far, stream_grad, wx, lengths, offsets),
        ext_scratch
        + [pltpu.VMEM((ext, feats), F32)] * 2
        + [pltpu.VMEM((rows, feats), BF)],
        moved=10 * 2**20,
    )
    part, back, onward = call(
        cp_sum_kernel,
        (shape((half, wide), BF), shape(back.shape, BF), shape(onward.shape, BF)),
        [ANY] + [VMEM] * (cps + 2),
        (query_g, own, *cp_got, back, onward),
    )
    last = lax.ppermute(back, "cp", downward)
    first = lax.ppermute(onward, "cp", upward)
    key_grad, value_grad = call(
        join_kernel,
        (shape((rows, feats), BF),) * 2,
        [VMEM] * 4,
        (key_g, value_g, last, first),
    )
    if floors != 4:
        at = (lax.axis_index("dp") % 2) * half
        whole = lax.dynamic_update_slice(
            jnp.zeros((shard, width), F32), part[:, :width].astype(F32), (at, 0)
        )
        weight_grad = lax.psum(whole, "dp")
        conv_grad = lax.psum(conv, ("cp", "dp"))[:KW]
    else:
        mine = call(
            z_sum_kernel,
            shape((half, wide), F32),
            [ANY] + [VMEM] * floors,
            (key_grad, part, *over_z(part)),
        )
        weight_grad, conv_grad = call(
            final_kernel,
            (shape((shard, width), F32), shape((KW, width), F32)),
            [VMEM] * 2,
            (mine, over_core(mine)),
        )
    return (
        query_g[None],
        key_grad[None],
        value_grad[None],
        stream_grad[None],
        weight_grad,
        conv_grad,
    )


def solution(mesh):
    rows_spec = P("dp", "cp", None)
    return jax.shard_map(
        body,
        mesh=mesh,
        in_specs=(rows_spec,) * 5 + (P("cp", None), P(), P("dp"), P("dp", None)),
        out_specs=(rows_spec,) * 4 + (P("cp", None), P()),
        check_vma=False,
    )
```

```python
import functools

import jax
import jax.numpy as jnp
from jax import lax
from jax.experimental import pallas as pl
from jax.experimental.pallas import tpu as pltpu
from jax.sharding import PartitionSpec as P

HEADS = 8
HSZ = 64
BLK = 24
KW = 7
HALF = KW // 2
BACK = 2 * BLK
AHEAD = 32
EDGE = 16
TILE = 4 * BLK
REACH = 176
GROUP = 4
FEATS = GROUP * HSZ
LANES = GROUP * TILE
NEG = -1e30
BF = jnp.bfloat16
F32 = jnp.float32
VMEM = pl.BlockSpec(memory_space=pltpu.VMEM)
ANY = pl.BlockSpec(memory_space=pl.ANY)


def nt(a, b):
    return lax.dot_general(a, b, (((1,), (1,)), ((), ())), preferred_element_type=F32)


def nn(a, b):
    return lax.dot_general(a, b, (((1,), (0,)), ((), ())), preferred_element_type=F32)


def tn(a, b):
    return lax.dot_general(a, b, (((0,), (0,)), ((), ())), preferred_element_type=F32)


def call(kernel, outs, ins, args, scratch=(), flops=0, moved=0):
    return pl.pallas_call(
        kernel,
        out_shape=outs,
        in_specs=ins,
        out_specs=jax.tree.map(lambda _: VMEM, outs),
        scratch_shapes=scratch,
        compiler_params=pltpu.CompilerParams(vmem_limit_bytes=40 * 1024 * 1024),
        cost_estimate=pl.CostEstimate(flops=flops, bytes_accessed=moved, transcendentals=0),
    )(*args)


def shape(dims, kind):
    return jax.ShapeDtypeStruct(dims, kind)


def pack_kernel(k, v, g, ahead, behind, edge, first, sems):
    rows = k.shape[0]
    feats = k.shape[1]
    pairs = [
        (k.at[pl.ds(rows - BACK, BACK)], ahead.at[pl.ds(0, BACK)]),
        (v.at[pl.ds(rows - BACK, BACK)], ahead.at[pl.ds(BACK, BACK)]),
        (k.at[pl.ds(0, AHEAD)], first.at[0]),
        (v.at[pl.ds(0, AHEAD)], first.at[1]),
        (g.at[pl.ds(rows - EDGE, EDGE)], edge.at[0]),
        (g.at[pl.ds(0, EDGE)], edge.at[1]),
    ]
    copies = [pltpu.make_async_copy(a, b, sems.at[i]) for i, (a, b) in enumerate(pairs)]
    for copy in copies:
        copy.start()
    for copy in copies:
        copy.wait()
    behind[0 : 2 * BLK] = jnp.concatenate(
        [first[0].astype(F32)[:BLK], first[1].astype(F32)[:BLK]], 0
    ).astype(BF)
    for out, block in ((ahead, edge[0].astype(F32)[8:]), (behind, edge[1].astype(F32)[:8])):
        two = jnp.concatenate([block[:, :feats], block[:, feats:]], 0)
        out[out.shape[0] - EDGE :] = two.astype(BF)


def packed(k, v, g):
    feats = k.shape[1]
    outs = (
        pltpu.VMEM((2 * BACK + EDGE, feats), BF),
        pltpu.VMEM((2 * BLK + EDGE, feats), BF),
    )
    return pl.pallas_call(
        pack_kernel,
        out_shape=outs,
        in_specs=[ANY] * 3,
        out_specs=(VMEM,) * 2,
        scratch_shapes=[
            pltpu.VMEM((2, EDGE, g.shape[1]), BF),
            pltpu.VMEM((2, AHEAD, feats), BF),
            pltpu.SemaphoreType.DMA((6,)),
        ],
        compiler_params=pltpu.CompilerParams(vmem_limit_bytes=40 * 1024 * 1024),
    )(*[pltpu.with_memory_space_constraint(x, pltpu.HBM) for x in (k, v, g)])


def head_of(dims):
    return lax.broadcasted_iota(jnp.int32, dims, 1) // HSZ


def stacked(tile, amount):
    head = head_of((1, FEATS))
    return jnp.concatenate(
        [tile * jnp.where(head == h, amount, 0.0).astype(BF) for h in range(GROUP)], 0
    )


def unstacked(product):
    head = head_of((TILE, FEATS))
    out = product[:TILE]
    for h in range(1, GROUP):
        out = jnp.where(head == h, product[h * TILE : (h + 1) * TILE], out)
    return out


def fill_ext(kx, vx, k, v, near, far):
    rows = k.shape[0]
    for at, ext, local in ((0, kx, k), (1, vx, v)):
        ext[0:BACK] = near[at * BACK : (at + 1) * BACK]
        ext[BACK : BACK + rows] = local[...]
        after = far[0 : 2 * BLK].astype(F32)[at * BLK : (at + 1) * BLK]
        zeros = jnp.zeros((AHEAD - BLK, after.shape[1]), F32)
        ext[BACK + rows :] = jnp.concatenate([after, zeros], 0).astype(BF)


def allowed_in(tile, base, length, back, ahead):
    lane = lax.broadcasted_iota(jnp.int32, (1, LANES), 1)
    within = lane
    for h in range(1, GROUP):
        within = within - jnp.where(lane >= h * TILE, TILE, 0)
    block = jnp.zeros_like(lane)
    for b in range(1, TILE // BLK):
        block = block + jnp.where(within >= b * BLK, 1, 0)
    origin = base + tile * TILE - BACK
    low = jnp.maximum((block + 2 - back) * BLK, -origin)
    high = jnp.minimum((block + 3 + ahead) * BLK, length - origin)
    row = lax.broadcasted_iota(jnp.int32, (REACH, LANES), 0)
    return (row >= low) & (row < high)


def probabilities(key_tile, query_stack, allowed):
    scores = jnp.where(allowed, nt(key_tile, query_stack), NEG)
    terms = jnp.exp(scores - jnp.max(scores, axis=0, keepdims=True))
    return terms * (1.0 / jnp.sum(terms, axis=0, keepdims=True))


def masked(block, start, length):
    frame = start + lax.broadcasted_iota(jnp.int32, block.shape, 0)
    return jnp.where((frame >= 0) & (frame < length), block.astype(F32), 0.0)


def fill_rims(gx, at, near, far, base, rows, length):
    feats = near.shape[1]
    before = near[2 * BACK :].astype(F32)
    after = far[2 * BLK :].astype(F32)
    for part in range(2):
        cols = slice(part * feats, (part + 1) * feats)
        here = slice(part * 8, (part + 1) * 8)
        gx[0:8, cols] = masked(before[here], base - 8, length)
        gx[at : at + 8, cols] = masked(after[here], base + rows, length)


def convolve(out, out_at, gx, gx_at, taps, start, count, length):
    width = out.shape[1]
    step = 128
    frame = start + lax.broadcasted_iota(jnp.int32, (count, step), 0)
    for at in range(0, width, step):
        cols = slice(at, at + step)
        total = taps[0:1, cols] * gx[gx_at + HALF : gx_at + HALF + count, cols]
        for tap in range(1, KW):
            top = gx_at + HALF - tap
            total = total + taps[tap : tap + 1, cols] * gx[top : top + count, cols]
        out[out_at : out_at + count, cols] = jnp.where(frame < length, total, 0.0).astype(BF)


def inner_conv_kernel(g, taps, w, lengths, offsets, out, w_half, gx):
    rows = g.shape[0]
    base = lax.axis_index("cp") * rows
    half = w.shape[0] // 2
    core = lax.rem(lax.axis_index("dp"), 2)
    w_half[...] = w[pl.ds(pl.multiple_of(core * half, half), half)]
    gx[0:8] = jnp.zeros((8, gx.shape[1]), F32)
    gx[8 + rows :] = jnp.zeros((8, gx.shape[1]), F32)
    length = lengths[...]
    gx[8 : 8 + rows] = masked(g[...], base, length)
    convolve(out, 0, gx, 8, taps, base, rows, length)


def forward_kernel(
    q, k, v, near, far, g, taps, inner, lengths, offsets,
    stream_grad, send, keep, att_out, kx, vx, gx, att_t,
):
    rows, feats = q.shape
    place = lax.axis_index("cp")
    core = lax.rem(lax.axis_index("dp"), 2)
    base = place * rows
    length = lengths[...]
    fill_ext(kx, vx, k, v, near, far)
    for tile in range(rows // TILE):
        start = tile * TILE
        allowed = allowed_in(tile, base, length, offsets[:, 0:1], offsets[:, 1:2])
        frame = base + start + lax.broadcasted_iota(jnp.int32, (TILE, FEATS), 0)
        for group in range(feats // FEATS):
            cols = slice(group * FEATS, (group + 1) * FEATS)
            query_stack = stacked(q[start : start + TILE, cols], HSZ**-0.5)
            probs = probabilities(kx[start : start + REACH, cols], query_stack, allowed)
            product = tn(probs.astype(BF), vx[start : start + REACH, cols])
            attended = jnp.where(frame < length, unstacked(product), 0.0).astype(BF)
            att_out[start : start + TILE, cols] = attended
    att_t[...] = att_out[...].astype(F32).T.astype(BF)
    fill_rims(gx, 56, near, far, base, rows, length)
    gx[8:32] = masked(g[0:32].astype(F32)[:24], base, length)
    gx[32:56] = masked(g[rows - 32 :].astype(F32)[8:], base + rows - 24, length)
    stream_grad[EDGE : rows - EDGE] = inner[EDGE : rows - EDGE]
    convolve(stream_grad, 0, gx, 8, taps, base, EDGE, length)
    convolve(stream_grad, rows - EDGE, gx, 40, taps, base + rows - EDGE, EDGE, length)
    half = send.shape[1]
    for part in range(send.shape[0]):
        there = pl.multiple_of(2 * half * part + half * (1 - core), half)
        here = pl.multiple_of(2 * half * part + half * core, half)
        send[part] = nn(att_t[pl.ds(there, half)], stream_grad[...]).astype(BF)
        keep[part] = nn(att_t[pl.ds(here, half)], stream_grad[...])


def folded(conv, half):
    extra = 8 * conv.shape[1] // half
    return jnp.concatenate(
        [conv[:, at : at + extra] for at in range(0, conv.shape[1], extra)], 0
    )


def split_kernel(keep, got, conv, own, *pieces):
    place = lax.axis_index("cp")
    half, width = keep.shape[1:]
    tail = folded(conv[...], half).astype(BF)
    own[:, :width] = keep[place] + got[place].astype(F32)
    own[:, width:] = tail.astype(F32)
    for by, piece in enumerate(pieces, 1):
        at = lax.bitwise_xor(place, by)
        piece[:, :width] = (keep[at] + got[at].astype(F32)).astype(BF)
        piece[:, width:] = tail


def tree_sum(terms):
    while len(terms) > 1:
        terms = [a + b for a, b in zip(terms[::2], terms[1::2])]
    return terms[0]


def cp_sum_kernel(after, back, onward, *refs):
    got = refs[:-3]
    part, back_out, onward_out = refs[-3:]
    part[...] = tree_sum([ref[...].astype(F32) for ref in got]).astype(BF)
    back_out[...] = back[...]
    onward_out[...] = onward[...]


def z_sum_kernel(after, *refs):
    refs[-1][...] = tree_sum([ref[...].astype(F32) for ref in refs[:-1]])


def final_kernel(after, mine, theirs, weight_grad, conv_grad):
    half = mine.shape[0]
    width = weight_grad.shape[1]
    core = lax.rem(lax.axis_index("dp"), 2)
    weight_grad[pl.ds(pl.multiple_of(core * half, half), half)] = mine[:, :width]
    weight_grad[pl.ds(pl.multiple_of((1 - core) * half, half), half)] = theirs[:, :width]
    extra = mine.shape[1] - width
    total = mine[:, width:] + theirs[:, width:]
    for at in range(0, half, 8):
        cols = slice(at // 8 * extra, (at // 8 + 1) * extra)
        conv_grad[:, cols] = total[at : at + KW]


def weight_stack_kernel(after, *refs):
    for k, ref in enumerate(refs[:-1]):
        refs[-1][k] = ref[...]


def conv_kernel(att, w, passed, stream, g, near, far, lengths, *refs):
    got = refs[:-4]
    conv, wx, gx, mixed = refs[-4:]
    rows, width = g.shape
    place = lax.axis_index("cp")
    core = lax.rem(lax.axis_index("dp"), 2)
    base = place * rows
    length = lengths[...]
    shard = w.shape[0]
    half = shard // 2
    wx[pl.ds(pl.multiple_of(place * shard, shard), shard)] = w[...]
    for by, ref in enumerate(got, 1):
        at = lax.bitwise_xor(place, by) * shard
        wx[pl.ds(pl.multiple_of(at + core * half, half), half)] = ref[...]
        wx[pl.ds(pl.multiple_of(at + (1 - core) * half, half), half)] = passed[by - 1]
    fill_rims(gx, 8 + rows, near, far, base, rows, length)
    gx[8 : 8 + rows] = masked(g[...], base, length)
    total = stream[...].astype(F32) + nn(att[...], wx[...])
    mixed[...] = masked(total, base, length)
    conv[KW:] = jnp.zeros((8 - KW, width), F32)
    step = 128
    for at in range(0, width, step):
        cols = slice(at, at + step)
        block = mixed[:, cols]
        for tap in range(KW):
            top = 8 + HALF - tap
            conv[tap : tap + 1, cols] = jnp.sum(
                block * gx[top : top + rows, cols], axis=0, keepdims=True
            )


def backward_kernel(
    after, q, k, v, near, far, stream_grad, wx, lengths, offsets,
    query_g, key_g, value_g, back, onward, token, kx, vx, kg, vg, ag,
):
    rows, feats = q.shape
    base = lax.axis_index("cp") * rows
    length = lengths[...]
    ag[...] = nt(stream_grad[...], wx[...]).astype(BF)
    fill_ext(kx, vx, k, v, near, far)
    kg[...] = jnp.zeros_like(kg)
    vg[...] = jnp.zeros_like(vg)
    for tile in range(rows // TILE):
        start = tile * TILE
        allowed = allowed_in(tile, base, length, offsets[:, 0:1], offsets[:, 1:2])
        span = slice(start, start + REACH)
        for group in range(feats // FEATS):
            cols = slice(group * FEATS, (group + 1) * FEATS)
            query_stack = stacked(q[start : start + TILE, cols], HSZ**-0.5)
            grad_stack = stacked(ag[start : start + TILE, cols], 1.0)
            probs = probabilities(kx[span, cols], query_stack, allowed)
            dprob = nt(vx[span, cols], grad_stack)
            inner = jnp.sum(probs * dprob, axis=0, keepdims=True)
            dscore = (probs * (dprob - inner)).astype(BF)
            query_g[start : start + TILE, cols] = (
                unstacked(tn(dscore, kx[span, cols])) * HSZ**-0.5
            ).astype(BF)
            kg[span, cols] += nn(dscore, query_stack)
            vg[span, cols] += nn(probs.astype(BF), grad_stack)
    key_g[...] = kg[BACK : BACK + rows]
    value_g[...] = vg[BACK : BACK + rows]
    for at, ext in ((0, kg), (1, vg)):
        back[at * BACK : (at + 1) * BACK] = ext[0:BACK].astype(BF)
    span = slice(BACK + rows, BACK + rows + BLK)
    onward[...] = jnp.concatenate([kg[span], vg[span]], 0).astype(BF)
    token[...] = jnp.zeros_like(token)


def join_kernel(key_g, value_g, last, first, key_out, value_out, token):
    rows = key_g.shape[0]
    for at, grad, out in ((0, key_g, key_out), (1, value_g, value_out)):
        before = first[...].astype(F32)[at * BLK : (at + 1) * BLK]
        zeros = jnp.zeros((AHEAD - BLK, before.shape[1]), F32)
        out[0:AHEAD] = (grad[0:AHEAD] + jnp.concatenate([before, zeros], 0)).astype(BF)
        out[AHEAD : rows - BACK] = grad[AHEAD : rows - BACK].astype(BF)
        out[rows - BACK :] = (
            grad[rows - BACK :] + last[at * BACK : (at + 1) * BACK].astype(F32)
        ).astype(BF)
    token[...] = jnp.zeros_like(token)


def body(
    queries, key_rows, value_rows, stream_in, out_grad, out_weight, conv_weight, lengths, offsets
):
    rows, feats = queries.shape[1:]
    width = stream_in.shape[2]
    cps, dps = lax.axis_size("cp"), lax.axis_size("dp")
    floors = dps // 2
    q, k, v, g, stream = queries[0], key_rows[0], value_rows[0], out_grad[0], stream_in[0]
    shard = out_weight.shape[0]
    half = shard // 2
    lengths = lengths.reshape(1, 1)
    ext = rows + BACK + AHEAD
    upward = [(i, (i + 1) % cps) for i in range(cps)]
    downward = [(i, (i - 1) % cps) for i in range(cps)]

    def over_cp(arrays):
        return [
            lax.ppermute(array, "cp", [(i, i ^ by) for i in range(cps)])
            for by, array in enumerate(arrays, 1)
        ]

    def over_z(array):
        return [
            lax.ppermute(array, "dp", [(i, i ^ (2 * by)) for i in range(dps)])
            for by in range(1, floors)
        ]

    def over_core(array):
        return lax.ppermute(array, "dp", [(i, i ^ 1) for i in range(dps)])

    ahead, behind = packed(k, v, g)
    near = lax.ppermute(ahead, "cp", upward)
    far = lax.ppermute(behind, "cp", downward)
    inner, w_half = call(
        inner_conv_kernel,
        (shape((rows, width), BF), shape((half, width), BF)),
        [VMEM] * 5,
        (g, conv_weight, out_weight, lengths, offsets),
        [pltpu.VMEM((rows + 16, width), F32)],
    )
    w_got = over_cp([w_half] * (cps - 1))
    ext_scratch = [pltpu.VMEM((ext, feats), BF)] * 2
    stream_grad, send, keep, att = call(
        forward_kernel,
        (
            shape((rows, width), BF),
            shape((cps, half, width), BF),
            shape((cps, half, width), F32),
            shape((rows, feats), BF),
        ),
        [VMEM] * 10,
        (q, k, v, near, far, g, conv_weight, inner, lengths, offsets),
        ext_scratch + [pltpu.VMEM((64, width), F32), pltpu.VMEM((feats, rows), BF)],
    )
    core_got = over_core(send)
    passed = over_core(
        call(
            weight_stack_kernel,
            shape((cps - 1, half, width), BF),
            [ANY] + [VMEM] * (cps - 1),
            (att, *w_got),
        )
    )
    conv, wx = call(
        conv_kernel,
        (shape((8, width), F32), shape((feats, width), BF)),
        [VMEM] * (7 + cps),
        (att, out_weight, passed, stream, g, near, far, lengths, *w_got),
        [pltpu.VMEM((rows + 16, width), F32), pltpu.VMEM((rows, width), F32)],
    )
    wide = width + 8 * width // half
    own, *pieces = call(
        split_kernel,
        (shape((half, wide), F32),) + (shape((half, wide), BF),) * (cps - 1),
        [VMEM] * 3,
        (keep, core_got, conv),
    )
    cp_got = over_cp(pieces)
    token = shape((8, 128), F32)
    query_g, key_g, value_g, back, onward, bwd_done = call(
        backward_kernel,
        (
            shape((rows, feats), BF),
            shape((rows, feats), F32),
            shape((rows, feats), F32),
            shape((2 * BACK, feats), BF),
            shape((2 * BLK, feats), BF),
            token,
        ),
        [ANY] + [VMEM] * 9,
        (own, q, k, v, near, far, stream_grad, wx, lengths, offsets),
        ext_scratch
        + [pltpu.VMEM((ext, feats), F32)] * 2
        + [pltpu.VMEM((rows, feats), BF)],
        moved=10 * 2**20,
    )
    part, back, onward = call(
        cp_sum_kernel,
        (shape((half, wide), BF), shape(back.shape, BF), shape(onward.shape, BF)),
        [VMEM] * (cps + 3),
        (bwd_done, back, onward, own, *cp_got),
    )
    last = lax.ppermute(back, "cp", downward)
    first = lax.ppermute(onward, "cp", upward)
    key_grad, value_grad, join_done = call(
        join_kernel,
        (shape((rows, feats), BF),) * 2 + (token,),
        [VMEM] * 4,
        (key_g, value_g, last, first),
    )
    if floors != 4:
        at = (lax.axis_index("dp") % 2) * half
        whole = lax.dynamic_update_slice(
            jnp.zeros((shard, width), F32), part[:, :width].astype(F32), (at, 0)
        )
        weight_grad = lax.psum(whole, "dp")
        conv_grad = lax.psum(conv, ("cp", "dp"))[:KW]
    else:
        mine = call(
            z_sum_kernel,
            shape((half, wide), F32),
            [VMEM] * (floors + 1),
            (join_done, part, *over_z(part)),
        )
        weight_grad, conv_grad = call(
            final_kernel,
            (shape((shard, width), F32), shape((KW, width), F32)),
            [VMEM] * 3,
            (join_done, mine, over_core(mine)),
        )
    return (
        query_g[None],
        key_grad[None],
        value_grad[None],
        stream_grad[None],
        weight_grad,
        conv_grad,
    )


def solution(mesh):
    rows_spec = P("dp", "cp", None)
    return jax.shard_map(
        body,
        mesh=mesh,
        in_specs=(rows_spec,) * 5 + (P("cp", None), P(), P("dp"), P("dp", None)),
        out_specs=(rows_spec,) * 4 + (P("cp", None), P()),
        check_vma=False,
    )
```

```python
import functools

import jax
import jax.numpy as jnp
from jax import lax
from jax.experimental import pallas as pl
from jax.experimental.pallas import tpu as pltpu
from jax.sharding import PartitionSpec as P

HEADS = 8
HSZ = 64
BLK = 24
KW = 7
HALF = KW // 2
BACK = 2 * BLK
AHEAD = 32
EDGE = 16
TILE = 4 * BLK
REACH = 176
GROUP = 4
FEATS = GROUP * HSZ
LANES = GROUP * TILE
NEG = -1e30
BF = jnp.bfloat16
F32 = jnp.float32
VMEM = pl.BlockSpec(memory_space=pltpu.VMEM)
ANY = pl.BlockSpec(memory_space=pl.ANY)


def nt(a, b):
    return lax.dot_general(a, b, (((1,), (1,)), ((), ())), preferred_element_type=F32)


def nn(a, b):
    return lax.dot_general(a, b, (((1,), (0,)), ((), ())), preferred_element_type=F32)


def tn(a, b):
    return lax.dot_general(a, b, (((0,), (0,)), ((), ())), preferred_element_type=F32)


def call(kernel, outs, ins, args, scratch=(), flops=0, moved=0):
    return pl.pallas_call(
        kernel,
        out_shape=outs,
        in_specs=ins,
        out_specs=jax.tree.map(lambda _: VMEM, outs),
        scratch_shapes=scratch,
        compiler_params=pltpu.CompilerParams(vmem_limit_bytes=40 * 1024 * 1024),
        cost_estimate=pl.CostEstimate(flops=flops, bytes_accessed=moved, transcendentals=0),
    )(*args)


def shape(dims, kind):
    return jax.ShapeDtypeStruct(dims, kind)


def half_cols(side, width):
    return pl.ds(pl.multiple_of(side * (width // 2), width // 2), width // 2)


def pack_kernel(
    k, v, g, w, lengths, offsets, ahead, behind, facts, w_half, edge, first, length, pair, sems,
):
    rows = k.shape[0]
    feats = k.shape[1]
    core = lax.rem(lax.axis_index("dp"), 2)
    pairs = [
        (k.at[pl.ds(rows - BACK, BACK)], ahead.at[pl.ds(0, BACK)]),
        (v.at[pl.ds(rows - BACK, BACK)], ahead.at[pl.ds(BACK, BACK)]),
        (k.at[pl.ds(0, AHEAD)], first.at[0]),
        (v.at[pl.ds(0, AHEAD)], first.at[1]),
        (g.at[pl.ds(rows - EDGE, EDGE)], edge.at[0]),
        (g.at[pl.ds(0, EDGE)], edge.at[1]),
        (w.at[:, half_cols(core, w.shape[1])], w_half),
        (lengths, length),
        (offsets, pair),
    ]
    copies = [pltpu.make_async_copy(a, b, sems.at[i]) for i, (a, b) in enumerate(pairs)]
    for copy in copies:
        copy.start()
    for copy in copies:
        copy.wait()
    for row, value in enumerate((length[0], pair[0, 0], pair[0, 1])):
        facts[row : row + 1] = jnp.full((1, facts.shape[1]), value, jnp.int32)
    behind[0 : 2 * BLK] = jnp.concatenate(
        [first[0].astype(F32)[:BLK], first[1].astype(F32)[:BLK]], 0
    ).astype(BF)
    for out, block in ((ahead, edge[0].astype(F32)[8:]), (behind, edge[1].astype(F32)[:8])):
        two = jnp.concatenate([block[:, :feats], block[:, feats:]], 0)
        out[out.shape[0] - EDGE :] = two.astype(BF)


def packed(*args):
    feats, width = args[0].shape[1], args[2].shape[1]
    outs = (
        pltpu.VMEM((2 * BACK + EDGE, feats), BF),
        pltpu.VMEM((2 * BLK + EDGE, feats), BF),
        pltpu.VMEM((8, 128), jnp.int32),
        pltpu.VMEM((args[3].shape[0], width // 2), BF),
    )
    return pl.pallas_call(
        pack_kernel,
        out_shape=outs,
        in_specs=[ANY] * 6,
        out_specs=(VMEM,) * 4,
        scratch_shapes=[
            pltpu.VMEM((2, EDGE, width), BF),
            pltpu.VMEM((2, AHEAD, feats), BF),
            pltpu.SMEM((1,), jnp.int32),
            pltpu.SMEM((1, 2), jnp.int32),
            pltpu.SemaphoreType.DMA((9,)),
        ],
        compiler_params=pltpu.CompilerParams(vmem_limit_bytes=40 * 1024 * 1024),
    )(*[x if x.ndim == 1 else pltpu.with_memory_space_constraint(x, pltpu.HBM) for x in args])


def head_of(dims):
    return lax.broadcasted_iota(jnp.int32, dims, 1) // HSZ


def stacked(tile, amount):
    head = head_of((1, FEATS))
    return jnp.concatenate(
        [tile * jnp.where(head == h, amount, 0.0).astype(BF) for h in range(GROUP)], 0
    )


def unstacked(product):
    head = head_of((TILE, FEATS))
    out = product[:TILE]
    for h in range(1, GROUP):
        out = jnp.where(head == h, product[h * TILE : (h + 1) * TILE], out)
    return out


def fill_ext(kx, vx, k, v, near, far):
    rows = k.shape[0]
    for at, ext, local in ((0, kx, k), (1, vx, v)):
        ext[0:BACK] = near[at * BACK : (at + 1) * BACK]
        ext[BACK : BACK + rows] = local[...]
        after = far[0 : 2 * BLK].astype(F32)[at * BLK : (at + 1) * BLK]
        zeros = jnp.zeros((AHEAD - BLK, after.shape[1]), F32)
        ext[BACK + rows :] = jnp.concatenate([after, zeros], 0).astype(BF)


def allowed_in(tile, base, length, back, ahead):
    lane = lax.broadcasted_iota(jnp.int32, (1, LANES), 1)
    within = lane
    for h in range(1, GROUP):
        within = within - jnp.where(lane >= h * TILE, TILE, 0)
    block = jnp.zeros_like(lane)
    for b in range(1, TILE // BLK):
        block = block + jnp.where(within >= b * BLK, 1, 0)
    origin = base + tile * TILE - BACK
    low = jnp.maximum((block + 2 - back) * BLK, -origin)
    high = jnp.minimum((block + 3 + ahead) * BLK, length - origin)
    row = lax.broadcasted_iota(jnp.int32, (REACH, LANES), 0)
    return (row >= low) & (row < high)


def probabilities(key_tile, query_stack, allowed):
    scores = jnp.where(allowed, nt(key_tile, query_stack), NEG)
    terms = jnp.exp(scores - jnp.max(scores, axis=0, keepdims=True))
    return terms * (1.0 / jnp.sum(terms, axis=0, keepdims=True))


def masked(block, start, length):
    frame = start + lax.broadcasted_iota(jnp.int32, block.shape, 0)
    return jnp.where((frame >= 0) & (frame < length), block.astype(F32), 0.0)


def fill_rims(gx, at, near, far, base, rows, length):
    feats = near.shape[1]
    before = near[2 * BACK :].astype(F32)
    after = far[2 * BLK :].astype(F32)
    for part in range(2):
        cols = slice(part * feats, (part + 1) * feats)
        here = slice(part * 8, (part + 1) * 8)
        gx[0:8, cols] = masked(before[here], base - 8, length)
        gx[at : at + 8, cols] = masked(after[here], base + rows, length)


def fill_half(gx, side, g, near, far, base, length):
    rows = g.shape[0]
    before = near[2 * BACK :].astype(F32)
    after = far[2 * BLK :].astype(F32)
    gx[0:8] = masked(jnp.where(side == 0, before[:8], before[8:]), base - 8, length)
    gx[8 : 8 + rows] = masked(g[:, half_cols(side, g.shape[1])], base, length)
    gx[8 + rows :] = masked(jnp.where(side == 0, after[:8], after[8:]), base + rows, length)


def convolve(out, out_at, gx, gx_at, taps, start, count, length):
    width = out.shape[1]
    step = 128
    frame = start + lax.broadcasted_iota(jnp.int32, (count, step), 0)
    for at in range(0, width, step):
        cols = slice(at, at + step)
        total = taps[0:1, cols] * gx[gx_at + HALF : gx_at + HALF + count, cols]
        for tap in range(1, KW):
            top = gx_at + HALF - tap
            total = total + taps[tap : tap + 1, cols] * gx[top : top + count, cols]
        out[out_at : out_at + count, cols] = jnp.where(frame < length, total, 0.0).astype(BF)


def inner_conv_kernel(g, taps, facts, out, gx):
    rows = g.shape[0]
    base = lax.axis_index("cp") * rows
    gx[0:8] = jnp.zeros((8, gx.shape[1]), F32)
    gx[8 + rows :] = jnp.zeros((8, gx.shape[1]), F32)
    length = facts[0:1, 0:1]
    gx[8 : 8 + rows] = masked(g[...], base, length)
    convolve(out, 0, gx, 8, taps, base, rows, length)


def forward_kernel(q, k, v, near, far, g, stream, facts, att_out, send, kx, vx, half_gx):
    rows, feats = q.shape
    width = g.shape[1]
    core = lax.rem(lax.axis_index("dp"), 2)
    base = lax.axis_index("cp") * rows
    length = facts[0:1, 0:1]
    fill_ext(kx, vx, k, v, near, far)
    for tile in range(rows // TILE):
        start = tile * TILE
        allowed = allowed_in(tile, base, length, facts[1:2, 0:1], facts[2:3, 0:1])
        frame = base + start + lax.broadcasted_iota(jnp.int32, (TILE, FEATS), 0)
        for group in range(feats // FEATS):
            cols = slice(group * FEATS, (group + 1) * FEATS)
            query_stack = stacked(q[start : start + TILE, cols], HSZ**-0.5)
            probs = probabilities(kx[start : start + REACH, cols], query_stack, allowed)
            product = tn(probs.astype(BF), vx[start : start + REACH, cols])
            attended = jnp.where(frame < length, unstacked(product), 0.0).astype(BF)
            att_out[start : start + TILE, cols] = attended
            send[start : start + TILE, cols] = attended
    send[rows : 2 * rows] = masked(stream[:, half_cols(1 - core, width)], base, length).astype(BF)
    fill_half(half_gx, 1 - core, g, near, far, base, length)
    send[2 * rows :] = half_gx[...].astype(BF)


def weights_kernel(att, near, far, g, taps, inner, facts, stream_grad, send, keep, gx, att_t):
    rows = att.shape[0]
    parts, half, width = keep.shape
    core = lax.rem(lax.axis_index("dp"), 2)
    base = lax.axis_index("cp") * rows
    length = facts[0:1, 0:1]
    turned = att[...].astype(F32).T.astype(BF)
    for part in range(parts):
        for side in range(2):
            at = jnp.where(core == side, parts * half, 0) + part * half
            att_t[pl.ds(pl.multiple_of(at, half), half)] = turned[
                (2 * part + side) * half : (2 * part + side + 1) * half
            ]
    fill_rims(gx, 56, near, far, base, rows, length)
    gx[8:32] = masked(g[0:32].astype(F32)[:24], base, length)
    gx[32:56] = masked(g[rows - 32 :].astype(F32)[8:], base + rows - 24, length)
    stream_grad[EDGE : rows - EDGE] = inner[EDGE : rows - EDGE]
    convolve(stream_grad, 0, gx, 8, taps, base, EDGE, length)
    convolve(stream_grad, rows - EDGE, gx, 40, taps, base + rows - EDGE, EDGE, length)
    product = nn(att_t[...], stream_grad[...])
    for part in range(parts):
        send[part] = product[part * half : (part + 1) * half].astype(BF)
        keep[part] = product[(parts + part) * half : (parts + part + 1) * half]


def packed_grads(rows, conv):
    cut = conv.shape[1] // 2
    blocks = [rows[at : at + 16] for at in range(0, rows.shape[0], 16)]
    return jnp.concatenate(blocks + [jnp.concatenate([conv[:, :cut], conv[:, cut:]], 0)], 1)


def split_kernel(keep, got, conv, own, *pieces):
    place = lax.axis_index("cp")
    parts, half, width = keep.shape
    for by in range(parts):
        at = lax.bitwise_xor(place, by)
        block = packed_grads(keep[at] + got[at].astype(F32), conv[...].astype(BF).astype(F32))
        if by == 0:
            own[...] = block
        else:
            pieces[by - 1][...] = block.astype(BF)


def tree_sum(terms):
    while len(terms) > 1:
        terms = [a + b for a, b in zip(terms[::2], terms[1::2])]
    return terms[0]


def cp_sum_kernel(after, back, onward, *refs):
    got = refs[:-3]
    part, back_out, onward_out = refs[-3:]
    part[...] = tree_sum([ref[...].astype(F32) for ref in got]).astype(BF)
    back_out[...] = back[...]
    onward_out[...] = onward[...]


def z_sum_kernel(after, *refs):
    refs[-1][...] = tree_sum([ref[...].astype(F32) for ref in refs[:-1]])


def final_kernel(after, mine, theirs, weight_grad, conv_grad):
    width = weight_grad.shape[1]
    half = weight_grad.shape[0] // 2
    cut = width // 4
    core = lax.rem(lax.axis_index("dp"), 2)
    for side, grads in ((core, mine), (1 - core, theirs)):
        for at in range(0, half, 16):
            block = grads[:, at // 16 * width : (at // 16 + 1) * width]
            weight_grad[pl.ds(pl.multiple_of(side * half + at, 16), 16)] = block
        conv = grads[:, half // 16 * width :]
        for part in range(2):
            cols = pl.ds(pl.multiple_of((2 * side + part) * cut, cut), cut)
            conv_grad[:, cols] = conv[8 * part : 8 * part + KW]


def weight_stack_kernel(after, *refs):
    for k, ref in enumerate(refs[:-1]):
        refs[-1][k] = ref[...]


def own_columns_kernel(after, w, *refs):
    wx = refs[-1]
    shard, width = w.shape
    place = lax.axis_index("cp")
    core = lax.rem(lax.axis_index("dp"), 2)
    wx[pl.ds(pl.multiple_of(place * shard, shard), shard)] = w[:, half_cols(core, width)]
    for by, ref in enumerate(refs[:-1], 1):
        at = lax.bitwise_xor(place, by) * shard
        wx[pl.ds(pl.multiple_of(at, shard), shard)] = ref[...]


def conv_kernel(att, wx, stream, g, near, far, facts, other, conv, gx, mixed):
    rows, width = g.shape
    core = lax.rem(lax.axis_index("dp"), 2)
    base = lax.axis_index("cp") * rows
    length = facts[0:1, 0:1]
    cols = half_cols(core, width)
    fill_half(gx.at[0], core, g, near, far, base, length)
    gx[1] = other[2 * rows :].astype(F32)
    mixed[0] = masked(stream[:, cols], base, length) + nn(att[...], wx[...])
    mixed[1] = other[rows : 2 * rows].astype(F32) + nn(other[0:rows], wx[...])
    conv[KW:] = jnp.zeros((8 - KW, conv.shape[1]), F32)
    step = 128
    for at in range(0, width // 2, step):
        here = slice(at, at + step)
        blocks = [mixed[0, :, here], mixed[1, :, here]]
        for tap in range(KW):
            first = 8 + HALF - tap
            conv[tap : tap + 1, here] = jnp.sum(
                blocks[0] * gx[0, first : first + rows, here]
                + blocks[1] * gx[1, first : first + rows, here],
                axis=0,
                keepdims=True,
            )


def backward_kernel(
    after, q, k, v, near, far, stream_grad, facts, w, passed, *refs
):
    got = refs[:-12]
    query_g, key_g, value_g, back, onward, token, kx, vx, kg, vg, ag, wx = refs[-12:]
    rows, feats = q.shape
    place = lax.axis_index("cp")
    core = lax.rem(lax.axis_index("dp"), 2)
    shard, width = w.shape
    wx[pl.ds(pl.multiple_of(place * shard, shard), shard)] = w[...]
    for by, ref in enumerate(got, 1):
        at = pl.ds(pl.multiple_of(lax.bitwise_xor(place, by) * shard, shard), shard)
        wx[at, half_cols(core, width)] = ref[...]
        wx[at, half_cols(1 - core, width)] = passed[by - 1]
    base = lax.axis_index("cp") * rows
    length = facts[0:1, 0:1]
    ag[...] = nt(stream_grad[...], wx[...]).astype(BF)
    fill_ext(kx, vx, k, v, near, far)
    kg[...] = jnp.zeros_like(kg)
    vg[...] = jnp.zeros_like(vg)
    for tile in range(rows // TILE):
        start = tile * TILE
        allowed = allowed_in(tile, base, length, facts[1:2, 0:1], facts[2:3, 0:1])
        span = slice(start, start + REACH)
        for group in range(feats // FEATS):
            cols = slice(group * FEATS, (group + 1) * FEATS)
            query_stack = stacked(q[start : start + TILE, cols], HSZ**-0.5)
            grad_stack = stacked(ag[start : start + TILE, cols], 1.0)
            probs = probabilities(kx[span, cols], query_stack, allowed)
            dprob = nt(vx[span, cols], grad_stack)
            inner = jnp.sum(probs * dprob, axis=0, keepdims=True)
            dscore = (probs * (dprob - inner)).astype(BF)
            query_g[start : start + TILE, cols] = (
                unstacked(tn(dscore, kx[span, cols])) * HSZ**-0.5
            ).astype(BF)
            kg[span, cols] += nn(dscore, query_stack)
            vg[span, cols] += nn(probs.astype(BF), grad_stack)
    key_g[...] = kg[BACK : BACK + rows]
    value_g[...] = vg[BACK : BACK + rows]
    for at, ext in ((0, kg), (1, vg)):
        back[at * BACK : (at + 1) * BACK] = ext[0:BACK].astype(BF)
    span = slice(BACK + rows, BACK + rows + BLK)
    onward[...] = jnp.concatenate([kg[span], vg[span]], 0).astype(BF)
    token[...] = jnp.zeros_like(token)


def join_kernel(key_g, value_g, last, first, key_out, value_out, token):
    rows = key_g.shape[0]
    for at, grad, out in ((0, key_g, key_out), (1, value_g, value_out)):
        before = first[...].astype(F32)[at * BLK : (at + 1) * BLK]
        zeros = jnp.zeros((AHEAD - BLK, before.shape[1]), F32)
        out[0:AHEAD] = (grad[0:AHEAD] + jnp.concatenate([before, zeros], 0)).astype(BF)
        out[AHEAD : rows - BACK] = grad[AHEAD : rows - BACK].astype(BF)
        out[rows - BACK :] = (
            grad[rows - BACK :] + last[at * BACK : (at + 1) * BACK].astype(F32)
        ).astype(BF)
    token[...] = jnp.zeros_like(token)


def body(
    queries, key_rows, value_rows, stream_in, out_grad, out_weight, conv_weight, lengths, offsets
):
    rows, feats = queries.shape[1:]
    width = stream_in.shape[2]
    cps, dps = lax.axis_size("cp"), lax.axis_size("dp")
    floors = dps // 2
    q, k, v, g, stream = queries[0], key_rows[0], value_rows[0], out_grad[0], stream_in[0]
    shard = out_weight.shape[0]
    half = shard // 2
    ext = rows + BACK + AHEAD
    upward = [(i, (i + 1) % cps) for i in range(cps)]
    downward = [(i, (i - 1) % cps) for i in range(cps)]

    def over_cp(arrays):
        got = [
            lax.ppermute(arrays[by - 1], "cp", [(i, i ^ by) for i in range(cps)])
            for by in range(cps - 1, 0, -1)
        ]
        return got[::-1]

    def over_z(array):
        got = [
            lax.ppermute(array, "dp", [(i, i ^ (2 * by)) for i in range(dps)])
            for by in range(floors - 1, 0, -1)
        ]
        return got[::-1]

    def over_core(array):
        return lax.ppermute(array, "dp", [(i, i ^ 1) for i in range(dps)])

    ahead, behind, facts, w_half = packed(k, v, g, out_weight, lengths, offsets)
    near = lax.ppermute(ahead, "cp", upward)
    far = lax.ppermute(behind, "cp", downward)
    inner = call(
        inner_conv_kernel,
        shape((rows, width), BF),
        [VMEM] * 3,
        (g, conv_weight, facts),
        [pltpu.VMEM((rows + 16, width), F32)],
    )
    w_got = over_cp([w_half] * (cps - 1))
    ext_scratch = [pltpu.VMEM((ext, feats), BF)] * 2
    att, conv_send = call(
        forward_kernel,
        (shape((rows, feats), BF), shape((3 * rows + 16, width // 2), BF)),
        [VMEM] * 8,
        (q, k, v, near, far, g, stream, facts),
        ext_scratch + [pltpu.VMEM((rows + 16, width // 2), F32)],
        flops=2**32,
    )
    conv_got = over_core(conv_send)
    stream_grad, send, keep = call(
        weights_kernel,
        (
            shape((rows, width), BF),
            shape((cps, half, width), BF),
            shape((cps, half, width), F32),
        ),
        [VMEM] * 7,
        (att, near, far, g, conv_weight, inner, facts),
        [pltpu.VMEM((64, width), F32), pltpu.VMEM((feats, rows), BF)],
    )
    core_got = over_core(send)
    w_cols = call(
        own_columns_kernel,
        shape((feats, width // 2), BF),
        [ANY] + [VMEM] * cps,
        (send, out_weight, *w_got),
        flops=2**34,
    )
    conv = call(
        conv_kernel,
        shape((8, width // 2), F32),
        [VMEM] * 8,
        (att, w_cols, stream, g, near, far, facts, conv_got),
        [
            pltpu.VMEM((2, rows + 16, width // 2), F32),
            pltpu.VMEM((2, rows, width // 2), F32),
        ],
    )
    wide = half // 16 * width + width // 4
    own, *pieces = call(
        split_kernel,
        (shape((16, wide), F32),) + (shape((16, wide), BF),) * (cps - 1),
        [VMEM] * 3,
        (keep, core_got, conv),
    )
    cp_got = over_cp(pieces)
    token = shape((8, 128), F32)
    passed = over_core(
        call(
            weight_stack_kernel,
            shape((cps - 1, shard, width // 2), BF),
            [ANY] + [VMEM] * (cps - 1),
            (own, *w_got),
        )
    )
    query_g, key_g, value_g, back, onward, bwd_done = call(
        backward_kernel,
        (
            shape((rows, feats), BF),
            shape((rows, feats), F32),
            shape((rows, feats), F32),
            shape((2 * BACK, feats), BF),
            shape((2 * BLK, feats), BF),
            token,
        ),
        [ANY] + [VMEM] * (8 + cps),
        (own, q, k, v, near, far, stream_grad, facts, out_weight, passed, *w_got),
        ext_scratch
        + [pltpu.VMEM((ext, feats), F32)] * 2
        + [pltpu.VMEM((rows, feats), BF), pltpu.VMEM((feats, width), BF)],
        moved=10 * 2**20,
    )
    part, back, onward = call(
        cp_sum_kernel,
        (shape((16, wide), BF), shape(back.shape, BF), shape(onward.shape, BF)),
        [VMEM] * (cps + 3),
        (bwd_done, back, onward, own, *cp_got),
    )
    last = lax.ppermute(back, "cp", downward)
    first = lax.ppermute(onward, "cp", upward)
    key_grad, value_grad, join_done = call(
        join_kernel,
        (shape((rows, feats), BF),) * 2 + (token,),
        [VMEM] * 4,
        (key_g, value_g, last, first),
    )
    if floors != 4:
        core = lax.axis_index("dp") % 2
        blocks = [part[:, at * width : (at + 1) * width] for at in range(half // 16)]
        summed = jnp.concatenate(blocks, 0).astype(F32)
        weights = lax.dynamic_update_slice(
            jnp.zeros((shard, width), F32), summed, (core * half, 0)
        )
        taps = lax.dynamic_update_slice(
            jnp.zeros((8, width), F32), conv, (0, core * (width // 2))
        )
        weight_grad = lax.psum(weights, "dp")
        conv_grad = lax.psum(taps, ("cp", "dp"))[:KW]
    else:
        mine = call(
            z_sum_kernel,
            shape((16, wide), F32),
            [VMEM] * (floors + 1),
            (join_done, part, *over_z(part)),
        )
        weight_grad, conv_grad = call(
            final_kernel,
            (shape((shard, width), F32), shape((KW, width), F32)),
            [VMEM] * 3,
            (join_done, mine, over_core(mine)),
        )
    return (
        query_g[None],
        key_grad[None],
        value_grad[None],
        stream_grad[None],
        weight_grad,
        conv_grad,
    )


def solution(mesh):
    rows_spec = P("dp", "cp", None)
    return jax.shard_map(
        body,
        mesh=mesh,
        in_specs=(rows_spec,) * 5 + (P("cp", None), P(), P("dp"), P("dp", None)),
        out_specs=(rows_spec,) * 4 + (P("cp", None), P()),
        check_vma=False,
    )
```

```python
import functools

import jax
import jax.numpy as jnp
from jax import lax
from jax.experimental import pallas as pl
from jax.experimental.pallas import tpu as pltpu
from jax.sharding import PartitionSpec as P

HEADS = 8
HSZ = 64
BLK = 24
KW = 7
HALF = KW // 2
BACK = 2 * BLK
AHEAD = 32
EDGE = 16
TILE = 4 * BLK
REACH = 176
GROUP = 4
FEATS = GROUP * HSZ
LANES = GROUP * TILE
NEG = -1e30
W_ORDER = (1, 2, 3)
CP_ORDER = (1, 2, 3)
Z_ORDER = (3, 1, 2)
BF = jnp.bfloat16
F32 = jnp.float32
VMEM = pl.BlockSpec(memory_space=pltpu.VMEM)
ANY = pl.BlockSpec(memory_space=pl.ANY)


def nt(a, b):
    return lax.dot_general(a, b, (((1,), (1,)), ((), ())), preferred_element_type=F32)


def nn(a, b):
    return lax.dot_general(a, b, (((1,), (0,)), ((), ())), preferred_element_type=F32)


def tn(a, b):
    return lax.dot_general(a, b, (((0,), (0,)), ((), ())), preferred_element_type=F32)


def call(kernel, outs, ins, args, scratch=(), flops=0, moved=0):
    return pl.pallas_call(
        kernel,
        out_shape=outs,
        in_specs=ins,
        out_specs=jax.tree.map(lambda _: VMEM, outs),
        scratch_shapes=scratch,
        compiler_params=pltpu.CompilerParams(vmem_limit_bytes=40 * 1024 * 1024),
        cost_estimate=pl.CostEstimate(flops=flops, bytes_accessed=moved, transcendentals=0),
    )(*args)


def shape(dims, kind):
    return jax.ShapeDtypeStruct(dims, kind)


def half_cols(side, width):
    return pl.ds(pl.multiple_of(side * (width // 2), width // 2), width // 2)


def pack_kernel(
    k, v, g, w, ahead, behind, w_half, edge, first, sems,
):
    rows = k.shape[0]
    feats = k.shape[1]
    core = lax.rem(lax.axis_index("dp"), 2)
    pairs = [
        (k.at[pl.ds(rows - BACK, BACK)], ahead.at[pl.ds(0, BACK)]),
        (v.at[pl.ds(rows - BACK, BACK)], ahead.at[pl.ds(BACK, BACK)]),
        (k.at[pl.ds(0, AHEAD)], first.at[0]),
        (v.at[pl.ds(0, AHEAD)], first.at[1]),
        (g.at[pl.ds(rows - EDGE, EDGE)], edge.at[0]),
        (g.at[pl.ds(0, EDGE)], edge.at[1]),
        (w.at[:, half_cols(core, w.shape[1])], w_half),
    ]
    copies = [pltpu.make_async_copy(a, b, sems.at[i]) for i, (a, b) in enumerate(pairs)]
    for copy in copies:
        copy.start()
    for copy in copies:
        copy.wait()
    behind[0 : 2 * BLK] = jnp.concatenate(
        [first[0].astype(F32)[:BLK], first[1].astype(F32)[:BLK]], 0
    ).astype(BF)
    for out, block in ((ahead, edge[0].astype(F32)[8:]), (behind, edge[1].astype(F32)[:8])):
        two = jnp.concatenate([block[:, :feats], block[:, feats:]], 0)
        out[out.shape[0] - EDGE :] = two.astype(BF)


def packed(*args):
    feats, width = args[0].shape[1], args[2].shape[1]
    outs = (
        pltpu.VMEM((2 * BACK + EDGE, feats), BF),
        pltpu.VMEM((2 * BLK + EDGE, feats), BF),
        pltpu.VMEM((args[3].shape[0], width // 2), BF),
    )
    return pl.pallas_call(
        pack_kernel,
        out_shape=outs,
        in_specs=[ANY] * 4,
        out_specs=(VMEM,) * 3,
        scratch_shapes=[
            pltpu.VMEM((2, EDGE, width), BF),
            pltpu.VMEM((2, AHEAD, feats), BF),
            pltpu.SemaphoreType.DMA((7,)),
        ],
        compiler_params=pltpu.CompilerParams(vmem_limit_bytes=40 * 1024 * 1024),
    )(*[pltpu.with_memory_space_constraint(x, pltpu.HBM) for x in args])


def head_of(dims):
    return lax.broadcasted_iota(jnp.int32, dims, 1) // HSZ


def stacked(tile, amount):
    head = head_of((1, FEATS))
    return jnp.concatenate(
        [tile * jnp.where(head == h, amount, 0.0).astype(BF) for h in range(GROUP)], 0
    )


def unstacked(product):
    head = head_of((TILE, FEATS))
    out = product[:TILE]
    for h in range(1, GROUP):
        out = jnp.where(head == h, product[h * TILE : (h + 1) * TILE], out)
    return out


def fill_ext(kx, vx, k, v, near, far):
    rows = k.shape[0]
    for at, ext, local in ((0, kx, k), (1, vx, v)):
        ext[0:BACK] = near[at * BACK : (at + 1) * BACK]
        ext[BACK : BACK + rows] = local[...]
        after = far[0 : 2 * BLK].astype(F32)[at * BLK : (at + 1) * BLK]
        zeros = jnp.zeros((AHEAD - BLK, after.shape[1]), F32)
        ext[BACK + rows :] = jnp.concatenate([after, zeros], 0).astype(BF)


def allowed_in(tile, base, length, back, ahead):
    lane = lax.broadcasted_iota(jnp.int32, (1, LANES), 1)
    within = lane
    for h in range(1, GROUP):
        within = within - jnp.where(lane >= h * TILE, TILE, 0)
    block = jnp.zeros_like(lane)
    for b in range(1, TILE // BLK):
        block = block + jnp.where(within >= b * BLK, 1, 0)
    origin = base + tile * TILE - BACK
    low = jnp.maximum((block + 2 - back) * BLK, -origin)
    high = jnp.minimum((block + 3 + ahead) * BLK, length - origin)
    row = lax.broadcasted_iota(jnp.int32, (REACH, LANES), 0)
    return (row >= low) & (row < high)


def probabilities(key_tile, query_stack, allowed):
    scores = jnp.where(allowed, nt(key_tile, query_stack), NEG)
    terms = jnp.exp(scores - jnp.max(scores, axis=0, keepdims=True))
    return terms * (1.0 / jnp.sum(terms, axis=0, keepdims=True))


def masked(block, start, length):
    frame = start + lax.broadcasted_iota(jnp.int32, block.shape, 0)
    return jnp.where((frame >= 0) & (frame < length), block.astype(F32), 0.0)


def fill_rims(gx, at, near, far, base, rows, length):
    feats = near.shape[1]
    before = near[2 * BACK :].astype(F32)
    after = far[2 * BLK :].astype(F32)
    for part in range(2):
        cols = slice(part * feats, (part + 1) * feats)
        here = slice(part * 8, (part + 1) * 8)
        gx[0:8, cols] = masked(before[here], base - 8, length)
        gx[at : at + 8, cols] = masked(after[here], base + rows, length)


def fill_half(gx, side, g, near, far, base, length):
    rows = g.shape[0]
    before = near[2 * BACK :].astype(F32)
    after = far[2 * BLK :].astype(F32)
    gx[0:8] = masked(jnp.where(side == 0, before[:8], before[8:]), base - 8, length)
    gx[8 : 8 + rows] = masked(g[:, half_cols(side, g.shape[1])], base, length)
    gx[8 + rows :] = masked(jnp.where(side == 0, after[:8], after[8:]), base + rows, length)


def convolve(out, out_at, gx, gx_at, taps, start, count, length):
    width = out.shape[1]
    step = 128
    frame = start + lax.broadcasted_iota(jnp.int32, (count, step), 0)
    for at in range(0, width, step):
        cols = slice(at, at + step)
        total = taps[0:1, cols] * gx[gx_at + HALF : gx_at + HALF + count, cols]
        for tap in range(1, KW):
            top = gx_at + HALF - tap
            total = total + taps[tap : tap + 1, cols] * gx[top : top + count, cols]
        out[out_at : out_at + count, cols] = jnp.where(frame < length, total, 0.0).astype(BF)


def inner_conv_kernel(g, taps, lengths, offsets, out, facts, gx, pair, sem):
    copy = pltpu.make_async_copy(offsets, pair, sem)
    copy.start()
    facts[0:1] = jnp.full((1, facts.shape[1]), lengths[0], jnp.int32)
    rows = g.shape[0]
    base = lax.axis_index("cp") * rows
    gx[0:8] = jnp.zeros((8, gx.shape[1]), F32)
    gx[8 + rows :] = jnp.zeros((8, gx.shape[1]), F32)
    length = facts[0:1, 0:1]
    gx[8 : 8 + rows] = masked(g[...], base, length)
    convolve(out, 0, gx, 8, taps, base, rows, length)
    copy.wait()
    for row in range(2):
        facts[row + 1 : row + 2] = jnp.full((1, facts.shape[1]), pair[0, row], jnp.int32)


def forward_kernel(q, k, v, near, far, g, stream, facts, att_out, send, kx, vx, half_gx):
    rows, feats = q.shape
    width = g.shape[1]
    core = lax.rem(lax.axis_index("dp"), 2)
    base = lax.axis_index("cp") * rows
    length = facts[0:1, 0:1]
    fill_ext(kx, vx, k, v, near, far)
    for tile in range(rows // TILE):
        start = tile * TILE
        allowed = allowed_in(tile, base, length, facts[1:2, 0:1], facts[2:3, 0:1])
        frame = base + start + lax.broadcasted_iota(jnp.int32, (TILE, FEATS), 0)
        for group in range(feats // FEATS):
            cols = slice(group * FEATS, (group + 1) * FEATS)
            query_stack = stacked(q[start : start + TILE, cols], HSZ**-0.5)
            probs = probabilities(kx[start : start + REACH, cols], query_stack, allowed)
            product = tn(probs.astype(BF), vx[start : start + REACH, cols])
            attended = jnp.where(frame < length, unstacked(product), 0.0).astype(BF)
            att_out[start : start + TILE, cols] = attended
            send[start : start + TILE, cols] = attended
    send[rows : 2 * rows] = masked(stream[:, half_cols(1 - core, width)], base, length).astype(BF)
    fill_half(half_gx, 1 - core, g, near, far, base, length)
    send[2 * rows :] = half_gx[...].astype(BF)


def weights_kernel(att, near, far, g, taps, inner, facts, stream_grad, send, keep, gx, att_t):
    rows = att.shape[0]
    parts, half, width = keep.shape
    core = lax.rem(lax.axis_index("dp"), 2)
    base = lax.axis_index("cp") * rows
    length = facts[0:1, 0:1]
    turned = att[...].astype(F32).T.astype(BF)
    for part in range(parts):
        for side in range(2):
            at = jnp.where(core == side, parts * half, 0) + part * half
            att_t[pl.ds(pl.multiple_of(at, half), half)] = turned[
                (2 * part + side) * half : (2 * part + side + 1) * half
            ]
    fill_rims(gx, 56, near, far, base, rows, length)
    gx[8:32] = masked(g[0:32].astype(F32)[:24], base, length)
    gx[32:56] = masked(g[rows - 32 :].astype(F32)[8:], base + rows - 24, length)
    stream_grad[EDGE : rows - EDGE] = inner[EDGE : rows - EDGE]
    convolve(stream_grad, 0, gx, 8, taps, base, EDGE, length)
    convolve(stream_grad, rows - EDGE, gx, 40, taps, base + rows - EDGE, EDGE, length)
    product = nn(att_t[...], stream_grad[...])
    for part in range(parts):
        send[part] = product[part * half : (part + 1) * half].astype(BF)
        keep[part] = product[(parts + part) * half : (parts + part + 1) * half]


def packed_grads(rows, conv):
    cut = conv.shape[1] // 2
    blocks = [rows[at : at + 16] for at in range(0, rows.shape[0], 16)]
    return jnp.concatenate(blocks + [jnp.concatenate([conv[:, :cut], conv[:, cut:]], 0)], 1)


def split_kernel(keep, got, conv, own, *pieces):
    place = lax.axis_index("cp")
    parts, half, width = keep.shape
    for by in range(parts):
        at = lax.bitwise_xor(place, by)
        block = packed_grads(keep[at] + got[at].astype(F32), conv[...].astype(BF).astype(F32))
        if by == 0:
            own[...] = block
        else:
            pieces[by - 1][...] = block.astype(BF)


def ordered(arrays, order):
    return [arrays[by - 1] for by in order] if len(arrays) == len(order) else arrays


def tree_sum(terms):
    while len(terms) > 1:
        terms = [a + b for a, b in zip(terms[::2], terms[1::2])]
    return terms[0]


def cp_sum_kernel(after, back, onward, *refs):
    got = refs[:-3]
    part, back_out, onward_out = refs[-3:]
    part[...] = tree_sum([ref[...].astype(F32) for ref in got]).astype(BF)
    back_out[...] = back[...]
    onward_out[...] = onward[...]


def z_sum_kernel(after, *refs):
    refs[-1][...] = tree_sum([ref[...].astype(F32) for ref in refs[:-1]])


def final_kernel(after, mine, theirs, weight_grad, conv_grad):
    width = weight_grad.shape[1]
    half = weight_grad.shape[0] // 2
    cut = width // 4
    core = lax.rem(lax.axis_index("dp"), 2)
    for side, grads in ((core, mine), (1 - core, theirs)):
        for at in range(0, half, 16):
            block = grads[:, at // 16 * width : (at // 16 + 1) * width]
            weight_grad[pl.ds(pl.multiple_of(side * half + at, 16), 16)] = block
        conv = grads[:, half // 16 * width :]
        for part in range(2):
            cols = pl.ds(pl.multiple_of((2 * side + part) * cut, cut), cut)
            conv_grad[:, cols] = conv[8 * part : 8 * part + KW]


def weight_stack_kernel(after, *refs):
    for k, ref in enumerate(refs[:-1]):
        refs[-1][k] = ref[...]


def own_columns_kernel(order, after, w, *refs):
    wx = refs[-1]
    shard, width = w.shape
    place = lax.axis_index("cp")
    core = lax.rem(lax.axis_index("dp"), 2)
    wx[pl.ds(pl.multiple_of(place * shard, shard), shard)] = w[:, half_cols(core, width)]
    for by, ref in zip(order, refs[:-1]):
        at = lax.bitwise_xor(place, by) * shard
        wx[pl.ds(pl.multiple_of(at, shard), shard)] = ref[...]


def conv_kernel(att, wx, stream, g, near, far, facts, other, conv, gx, mixed):
    rows, width = g.shape
    core = lax.rem(lax.axis_index("dp"), 2)
    base = lax.axis_index("cp") * rows
    length = facts[0:1, 0:1]
    cols = half_cols(core, width)
    fill_half(gx.at[0], core, g, near, far, base, length)
    gx[1] = other[2 * rows :].astype(F32)
    mixed[0] = masked(stream[:, cols], base, length) + nn(att[...], wx[...])
    mixed[1] = other[rows : 2 * rows].astype(F32) + nn(other[0:rows], wx[...])
    conv[KW:] = jnp.zeros((8 - KW, conv.shape[1]), F32)
    step = 128
    for at in range(0, width // 2, step):
        here = slice(at, at + step)
        blocks = [mixed[0, :, here], mixed[1, :, here]]
        for tap in range(KW):
            first = 8 + HALF - tap
            conv[tap : tap + 1, here] = jnp.sum(
                blocks[0] * gx[0, first : first + rows, here]
                + blocks[1] * gx[1, first : first + rows, here],
                axis=0,
                keepdims=True,
            )


def backward_kernel(
    after, q, k, v, near, far, stream_grad, facts, w, passed, *refs
):
    got = refs[:-12]
    query_g, key_g, value_g, back, onward, token, kx, vx, kg, vg, ag, wx = refs[-12:]
    rows, feats = q.shape
    place = lax.axis_index("cp")
    core = lax.rem(lax.axis_index("dp"), 2)
    shard, width = w.shape
    wx[pl.ds(pl.multiple_of(place * shard, shard), shard)] = w[...]
    for by, ref in enumerate(got, 1):
        at = pl.ds(pl.multiple_of(lax.bitwise_xor(place, by) * shard, shard), shard)
        wx[at, half_cols(core, width)] = ref[...]
        wx[at, half_cols(1 - core, width)] = passed[by - 1]
    base = lax.axis_index("cp") * rows
    length = facts[0:1, 0:1]
    ag[...] = nt(stream_grad[...], wx[...]).astype(BF)
    fill_ext(kx, vx, k, v, near, far)
    kg[...] = jnp.zeros_like(kg)
    vg[...] = jnp.zeros_like(vg)
    for tile in range(rows // TILE):
        start = tile * TILE
        allowed = allowed_in(tile, base, length, facts[1:2, 0:1], facts[2:3, 0:1])
        span = slice(start, start + REACH)
        for group in range(feats // FEATS):
            cols = slice(group * FEATS, (group + 1) * FEATS)
            query_stack = stacked(q[start : start + TILE, cols], HSZ**-0.5)
            grad_stack = stacked(ag[start : start + TILE, cols], 1.0)
            probs = probabilities(kx[span, cols], query_stack, allowed)
            dprob = nt(vx[span, cols], grad_stack)
            inner = jnp.sum(probs * dprob, axis=0, keepdims=True)
            dscore = (probs * (dprob - inner)).astype(BF)
            query_g[start : start + TILE, cols] = (
                unstacked(tn(dscore, kx[span, cols])) * HSZ**-0.5
            ).astype(BF)
            kg[span, cols] += nn(dscore, query_stack)
            vg[span, cols] += nn(probs.astype(BF), grad_stack)
    key_g[...] = kg[BACK : BACK + rows]
    value_g[...] = vg[BACK : BACK + rows]
    for at, ext in ((0, kg), (1, vg)):
        back[at * BACK : (at + 1) * BACK] = ext[0:BACK].astype(BF)
    span = slice(BACK + rows, BACK + rows + BLK)
    onward[...] = jnp.concatenate([kg[span], vg[span]], 0).astype(BF)
    token[...] = jnp.zeros_like(token)


def join_kernel(key_g, value_g, last, first, key_out, value_out, token):
    rows = key_g.shape[0]
    for at, grad, out in ((0, key_g, key_out), (1, value_g, value_out)):
        before = first[...].astype(F32)[at * BLK : (at + 1) * BLK]
        zeros = jnp.zeros((AHEAD - BLK, before.shape[1]), F32)
        out[0:AHEAD] = (grad[0:AHEAD] + jnp.concatenate([before, zeros], 0)).astype(BF)
        out[AHEAD : rows - BACK] = grad[AHEAD : rows - BACK].astype(BF)
        out[rows - BACK :] = (
            grad[rows - BACK :] + last[at * BACK : (at + 1) * BACK].astype(F32)
        ).astype(BF)
    token[...] = jnp.zeros_like(token)


def body(
    queries, key_rows, value_rows, stream_in, out_grad, out_weight, conv_weight, lengths, offsets
):
    rows, feats = queries.shape[1:]
    width = stream_in.shape[2]
    cps, dps = lax.axis_size("cp"), lax.axis_size("dp")
    floors = dps // 2
    q, k, v, g, stream = queries[0], key_rows[0], value_rows[0], out_grad[0], stream_in[0]
    shard = out_weight.shape[0]
    half = shard // 2
    ext = rows + BACK + AHEAD
    upward = [(i, (i + 1) % cps) for i in range(cps)]
    downward = [(i, (i - 1) % cps) for i in range(cps)]

    def over_cp(arrays, order):
        got = [
            lax.ppermute(arrays[by - 1], "cp", [(i, i ^ by) for i in range(cps)])
            for by in order
        ]
        return [got[order.index(by)] for by in range(1, cps)]

    def over_z(array):
        got = [
            lax.ppermute(array, "dp", [(i, i ^ (2 * by)) for i in range(dps)])
            for by in range(floors - 1, 0, -1)
        ]
        return got[::-1]

    def over_core(array):
        return lax.ppermute(array, "dp", [(i, i ^ 1) for i in range(dps)])

    ahead, behind, w_half = packed(k, v, g, out_weight)
    near = lax.ppermute(ahead, "cp", upward)
    far = lax.ppermute(behind, "cp", downward)
    inner, facts = call(
        inner_conv_kernel,
        (shape((rows, width), BF), shape((8, 128), jnp.int32)),
        [VMEM] * 2 + [pl.BlockSpec(memory_space=pltpu.SMEM), ANY],
        (g, conv_weight, lengths, pltpu.with_memory_space_constraint(offsets, pltpu.HBM)),
        [
            pltpu.VMEM((rows + 16, width), F32),
            pltpu.SMEM((1, 2), jnp.int32),
            pltpu.SemaphoreType.DMA,
        ],
    )
    falling, rising = list(range(cps - 1, 0, -1)), list(range(1, cps))
    w_got = over_cp([w_half] * (cps - 1), falling)
    ext_scratch = [pltpu.VMEM((ext, feats), BF)] * 2
    att, conv_send = call(
        forward_kernel,
        (shape((rows, feats), BF), shape((3 * rows + 16, width // 2), BF)),
        [VMEM] * 8,
        (q, k, v, near, far, g, stream, facts),
        ext_scratch + [pltpu.VMEM((rows + 16, width // 2), F32)],
        flops=2**32,
    )
    conv_got = over_core(conv_send)
    stream_grad, send, keep = call(
        weights_kernel,
        (
            shape((rows, width), BF),
            shape((cps, half, width), BF),
            shape((cps, half, width), F32),
        ),
        [VMEM] * 7,
        (att, near, far, g, conv_weight, inner, facts),
        [pltpu.VMEM((64, width), F32), pltpu.VMEM((feats, rows), BF)],
    )
    core_got = over_core(send)
    w_order = W_ORDER if cps == 4 else tuple(range(1, cps))
    w_cols = call(
        functools.partial(own_columns_kernel, w_order),
        shape((feats, width // 2), BF),
        [ANY] + [VMEM] * cps,
        (send, out_weight, *ordered(w_got, w_order)),
        flops=2**34,
    )
    conv = call(
        conv_kernel,
        shape((8, width // 2), F32),
        [VMEM] * 8,
        (att, w_cols, stream, g, near, far, facts, conv_got),
        [
            pltpu.VMEM((2, rows + 16, width // 2), F32),
            pltpu.VMEM((2, rows, width // 2), F32),
        ],
    )
    wide = half // 16 * width + width // 4
    own, *pieces = call(
        split_kernel,
        (shape((16, wide), F32),) + (shape((16, wide), BF),) * (cps - 1),
        [VMEM] * 3,
        (keep, core_got, conv),
    )
    cp_got = over_cp(pieces, rising)
    token = shape((8, 128), F32)
    passed = over_core(
        call(
            weight_stack_kernel,
            shape((cps - 1, shard, width // 2), BF),
            [ANY] + [VMEM] * (cps - 1),
            (own, *w_got),
        )
    )
    query_g, key_g, value_g, back, onward, bwd_done = call(
        backward_kernel,
        (
            shape((rows, feats), BF),
            shape((rows, feats), F32),
            shape((rows, feats), F32),
            shape((2 * BACK, feats), BF),
            shape((2 * BLK, feats), BF),
            token,
        ),
        [ANY] + [VMEM] * (8 + cps),
        (own, q, k, v, near, far, stream_grad, facts, out_weight, passed, *w_got),
        ext_scratch
        + [pltpu.VMEM((ext, feats), F32)] * 2
        + [pltpu.VMEM((rows, feats), BF), pltpu.VMEM((feats, width), BF)],
        moved=10 * 2**20,
    )
    part, back, onward = call(
        cp_sum_kernel,
        (shape((16, wide), BF), shape(back.shape, BF), shape(onward.shape, BF)),
        [VMEM] * (cps + 3),
        (bwd_done, back, onward, own, *ordered(cp_got, CP_ORDER)),
    )
    last = lax.ppermute(back, "cp", downward)
    first = lax.ppermute(onward, "cp", upward)
    key_grad, value_grad, join_done = call(
        join_kernel,
        (shape((rows, feats), BF),) * 2 + (token,),
        [VMEM] * 4,
        (key_g, value_g, last, first),
    )
    if floors != 4:
        core = lax.axis_index("dp") % 2
        blocks = [part[:, at * width : (at + 1) * width] for at in range(half // 16)]
        summed = jnp.concatenate(blocks, 0).astype(F32)
        weights = lax.dynamic_update_slice(
            jnp.zeros((shard, width), F32), summed, (core * half, 0)
        )
        taps = lax.dynamic_update_slice(
            jnp.zeros((8, width), F32), conv, (0, core * (width // 2))
        )
        weight_grad = lax.psum(weights, "dp")
        conv_grad = lax.psum(taps, ("cp", "dp"))[:KW]
    else:
        mine = call(
            z_sum_kernel,
            shape((16, wide), F32),
            [VMEM] * (floors + 1),
            (join_done, part, *ordered(over_z(part), Z_ORDER)),
        )
        weight_grad, conv_grad = call(
            final_kernel,
            (shape((shard, width), F32), shape((KW, width), F32)),
            [VMEM] * 3,
            (join_done, mine, over_core(mine)),
        )
    return (
        query_g[None],
        key_grad[None],
        value_grad[None],
        stream_grad[None],
        weight_grad,
        conv_grad,
    )


def solution(mesh):
    rows_spec = P("dp", "cp", None)
    return jax.shard_map(
        body,
        mesh=mesh,
        in_specs=(rows_spec,) * 5 + (P("cp", None), P(), P("dp"), P("dp", None)),
        out_specs=(rows_spec,) * 4 + (P("cp", None), P()),
        check_vma=False,
    )
```

```python
import functools

import jax
import jax.numpy as jnp
from jax import lax
from jax.experimental import pallas as pl
from jax.experimental.pallas import tpu as pltpu
from jax.sharding import PartitionSpec as P

HEADS = 8
HSZ = 64
BLK = 24
KW = 7
HALF = KW // 2
BACK = 2 * BLK
AHEAD = 32
EDGE = 16
TILE = 4 * BLK
REACH = 176
GROUP = 4
FEATS = GROUP * HSZ
LANES = GROUP * TILE
LANE = 128
NEG = -1e30
W_ORDER = (1, 2, 3)
CP_ORDER = (1, 2, 3)
Z_ORDER = (3, 1, 2)
BF = jnp.bfloat16
F32 = jnp.float32
VMEM = pl.BlockSpec(memory_space=pltpu.VMEM)
ANY = pl.BlockSpec(memory_space=pl.ANY)


def nt(a, b):
    return lax.dot_general(a, b, (((1,), (1,)), ((), ())), preferred_element_type=F32)


def nn(a, b):
    return lax.dot_general(a, b, (((1,), (0,)), ((), ())), preferred_element_type=F32)


def tn(a, b):
    return lax.dot_general(a, b, (((0,), (0,)), ((), ())), preferred_element_type=F32)


def call(kernel, outs, ins, args, scratch=(), flops=0, moved=0):
    return pl.pallas_call(
        kernel,
        out_shape=outs,
        in_specs=ins,
        out_specs=jax.tree.map(lambda _: VMEM, outs),
        scratch_shapes=scratch,
        compiler_params=pltpu.CompilerParams(vmem_limit_bytes=40 * 1024 * 1024),
        cost_estimate=pl.CostEstimate(flops=flops, bytes_accessed=moved, transcendentals=0),
    )(*args)


def shape(dims, kind):
    return jax.ShapeDtypeStruct(dims, kind)


def half_cols(side, width):
    return pl.ds(pl.multiple_of(side * (width // 2), width // 2), width // 2)


def pack_kernel(
    k, v, g, w, ahead, behind, w_half, edge, first, sems,
):
    rows = k.shape[0]
    feats = k.shape[1]
    core = lax.rem(lax.axis_index("dp"), 2)
    pairs = [
        (k.at[pl.ds(rows - BACK, BACK)], ahead.at[pl.ds(0, BACK)]),
        (v.at[pl.ds(rows - BACK, BACK)], ahead.at[pl.ds(BACK, BACK)]),
        (k.at[pl.ds(0, AHEAD)], first.at[0]),
        (v.at[pl.ds(0, AHEAD)], first.at[1]),
        (g.at[pl.ds(rows - EDGE, EDGE)], edge.at[0]),
        (g.at[pl.ds(0, EDGE)], edge.at[1]),
        (w.at[:, half_cols(core, w.shape[1])], w_half),
    ]
    copies = [pltpu.make_async_copy(a, b, sems.at[i]) for i, (a, b) in enumerate(pairs)]
    for copy in copies:
        copy.start()
    for copy in copies:
        copy.wait()
    behind[0 : 2 * BLK] = jnp.concatenate(
        [first[0].astype(F32)[:BLK], first[1].astype(F32)[:BLK]], 0
    ).astype(BF)
    for out, block in ((ahead, edge[0].astype(F32)[8:]), (behind, edge[1].astype(F32)[:8])):
        two = jnp.concatenate([block[:, :feats], block[:, feats:]], 0)
        out[out.shape[0] - EDGE :] = two.astype(BF)


def packed(*args):
    feats, width = args[0].shape[1], args[2].shape[1]
    outs = (
        pltpu.VMEM((2 * BACK + EDGE, feats), BF),
        pltpu.VMEM((2 * BLK + EDGE, feats), BF),
        pltpu.VMEM((args[3].shape[0], width // 2), BF),
    )
    return pl.pallas_call(
        pack_kernel,
        out_shape=outs,
        in_specs=[ANY] * 4,
        out_specs=(VMEM,) * 3,
        scratch_shapes=[
            pltpu.VMEM((2, EDGE, width), BF),
            pltpu.VMEM((2, AHEAD, feats), BF),
            pltpu.SemaphoreType.DMA((7,)),
        ],
        compiler_params=pltpu.CompilerParams(vmem_limit_bytes=40 * 1024 * 1024),
    )(*[pltpu.with_memory_space_constraint(x, pltpu.HBM) for x in args])


def head_of(dims):
    return lax.broadcasted_iota(jnp.int32, dims, 1) // HSZ


def stacked(tile, amount):
    head = head_of((1, FEATS))
    return jnp.concatenate(
        [tile * jnp.where(head == h, amount, 0.0).astype(BF) for h in range(GROUP)], 0
    )


def unstacked(product):
    head = head_of((TILE, FEATS))
    out = product[:TILE]
    for h in range(1, GROUP):
        out = jnp.where(head == h, product[h * TILE : (h + 1) * TILE], out)
    return out


def fill_ext(kx, vx, k, v, near, far):
    rows = k.shape[0]
    for at, ext, local in ((0, kx, k), (1, vx, v)):
        ext[0:BACK] = near[at * BACK : (at + 1) * BACK]
        ext[BACK : BACK + rows] = local[...]
        after = far[0 : 2 * BLK].astype(F32)[at * BLK : (at + 1) * BLK]
        zeros = jnp.zeros((AHEAD - BLK, after.shape[1]), F32)
        ext[BACK + rows :] = jnp.concatenate([after, zeros], 0).astype(BF)


def allowed_in(tile, base, length, back, ahead):
    lane = lax.broadcasted_iota(jnp.int32, (1, LANES), 1)
    within = lane
    for h in range(1, GROUP):
        within = within - jnp.where(lane >= h * TILE, TILE, 0)
    block = jnp.zeros_like(lane)
    for b in range(1, TILE // BLK):
        block = block + jnp.where(within >= b * BLK, 1, 0)
    origin = base + tile * TILE - BACK
    low = jnp.maximum((block + 2 - back) * BLK, -origin)
    high = jnp.minimum((block + 3 + ahead) * BLK, length - origin)
    row = lax.broadcasted_iota(jnp.int32, (REACH, LANES), 0)
    return (row >= low) & (row < high)


def probabilities(key_tile, query_stack, allowed):
    scores = jnp.where(allowed, nt(key_tile, query_stack), NEG)
    terms = jnp.exp(scores - jnp.max(scores, axis=0, keepdims=True))
    return terms * (1.0 / jnp.sum(terms, axis=0, keepdims=True))


def masked(block, start, length):
    frame = start + lax.broadcasted_iota(jnp.int32, block.shape, 0)
    return jnp.where((frame >= 0) & (frame < length), block.astype(F32), 0.0)


def put(gx, at, block):
    for chunk in range(gx.shape[0]):
        gx[chunk, at : at + block.shape[0]] = block[:, chunk * LANE : (chunk + 1) * LANE]


def rims(near, far, base, rows, length):
    before = near[2 * BACK :].astype(F32)
    after = far[2 * BLK :].astype(F32)
    return (
        masked(jnp.concatenate([before[:8], before[8:]], 1), base - 8, length),
        masked(jnp.concatenate([after[:8], after[8:]], 1), base + rows, length),
    )


def fill_half(gx, side, g, near, far, base, length):
    rows = g.shape[0]
    before = near[2 * BACK :].astype(F32)
    after = far[2 * BLK :].astype(F32)
    put(gx, 0, masked(jnp.where(side == 0, before[:8], before[8:]), base - 8, length))
    put(gx, 8, masked(g[:, half_cols(side, g.shape[1])], base, length))
    put(gx, 8 + rows, masked(jnp.where(side == 0, after[:8], after[8:]), base + rows, length))


def convolve(out, out_at, gx, gx_at, taps, start, count, length):
    frame = start + lax.broadcasted_iota(jnp.int32, (count, LANE), 0)
    for chunk in range(gx.shape[0]):
        cols = slice(chunk * LANE, (chunk + 1) * LANE)
        first = gx_at + HALF
        total = taps[0:1, cols] * gx[chunk, first : first + count]
        for tap in range(1, KW):
            first = gx_at + HALF - tap
            total = total + taps[tap : tap + 1, cols] * gx[chunk, first : first + count]
        out[out_at : out_at + count, cols] = jnp.where(frame < length, total, 0.0).astype(BF)


def inner_conv_kernel(g, taps, lengths, offsets, out, facts, gx, pair, sem):
    copy = pltpu.make_async_copy(offsets, pair, sem)
    copy.start()
    facts[0:1] = jnp.full((1, facts.shape[1]), lengths[0], jnp.int32)
    rows = g.shape[0]
    base = lax.axis_index("cp") * rows
    gx[:, 0:8] = jnp.zeros((gx.shape[0], 8, LANE), F32)
    gx[:, 8 + rows :] = jnp.zeros((gx.shape[0], 8, LANE), F32)
    length = facts[0:1, 0:1]
    put(gx, 8, masked(g[...], base, length))
    convolve(out, 0, gx, 8, taps, base, rows, length)
    copy.wait()
    for row in range(2):
        facts[row + 1 : row + 2] = jnp.full((1, facts.shape[1]), pair[0, row], jnp.int32)


def forward_kernel(q, k, v, near, far, g, stream, facts, att_out, send, kx, vx, half_gx):
    rows, feats = q.shape
    width = g.shape[1]
    core = lax.rem(lax.axis_index("dp"), 2)
    base = lax.axis_index("cp") * rows
    length = facts[0:1, 0:1]
    fill_ext(kx, vx, k, v, near, far)
    for tile in range(rows // TILE):
        start = tile * TILE
        allowed = allowed_in(tile, base, length, facts[1:2, 0:1], facts[2:3, 0:1])
        frame = base + start + lax.broadcasted_iota(jnp.int32, (TILE, FEATS), 0)
        for group in range(feats // FEATS):
            cols = slice(group * FEATS, (group + 1) * FEATS)
            query_stack = stacked(q[start : start + TILE, cols], HSZ**-0.5)
            probs = probabilities(kx[start : start + REACH, cols], query_stack, allowed)
            product = tn(probs.astype(BF), vx[start : start + REACH, cols])
            attended = jnp.where(frame < length, unstacked(product), 0.0).astype(BF)
            att_out[start : start + TILE, cols] = attended
            send[start : start + TILE, cols] = attended
    send[rows : 2 * rows] = masked(stream[:, half_cols(1 - core, width)], base, length).astype(BF)
    fill_half(half_gx, 1 - core, g, near, far, base, length)
    for chunk in range(half_gx.shape[0]):
        send[2 * rows :, chunk * LANE : (chunk + 1) * LANE] = half_gx[chunk].astype(BF)


def weights_kernel(att, near, far, g, taps, inner, facts, stream_grad, send, keep, gx, att_t):
    rows = att.shape[0]
    parts, half, width = keep.shape
    core = lax.rem(lax.axis_index("dp"), 2)
    base = lax.axis_index("cp") * rows
    length = facts[0:1, 0:1]
    turned = att[...].astype(F32).T.astype(BF)
    for part in range(parts):
        for side in range(2):
            at = jnp.where(core == side, parts * half, 0) + part * half
            att_t[pl.ds(pl.multiple_of(at, half), half)] = turned[
                (2 * part + side) * half : (2 * part + side + 1) * half
            ]
    before, after = rims(near, far, base, rows, length)
    put(gx, 0, before)
    put(gx, 8, masked(g[0:32].astype(F32)[:24], base, length))
    put(gx, 32, masked(g[rows - 32 :].astype(F32)[8:], base + rows - 24, length))
    put(gx, 56, after)
    stream_grad[EDGE : rows - EDGE] = inner[EDGE : rows - EDGE]
    convolve(stream_grad, 0, gx, 8, taps, base, EDGE, length)
    convolve(stream_grad, rows - EDGE, gx, 40, taps, base + rows - EDGE, EDGE, length)
    product = nn(att_t[...], stream_grad[...])
    for part in range(parts):
        send[part] = product[part * half : (part + 1) * half].astype(BF)
        keep[part] = product[(parts + part) * half : (parts + part + 1) * half]


def packed_grads(rows, conv):
    cut = conv.shape[1] // 2
    blocks = [rows[at : at + 16] for at in range(0, rows.shape[0], 16)]
    return jnp.concatenate(blocks + [jnp.concatenate([conv[:, :cut], conv[:, cut:]], 0)], 1)


def split_kernel(keep, got, conv, own, *pieces):
    place = lax.axis_index("cp")
    parts, half, width = keep.shape
    for by in range(parts):
        at = lax.bitwise_xor(place, by)
        block = packed_grads(keep[at] + got[at].astype(F32), conv[...].astype(BF).astype(F32))
        if by == 0:
            own[...] = block
        else:
            pieces[by - 1][...] = block.astype(BF)


def ordered(arrays, order):
    return [arrays[by - 1] for by in order] if len(arrays) == len(order) else arrays


def tree_sum(terms):
    while len(terms) > 1:
        terms = [a + b for a, b in zip(terms[::2], terms[1::2])]
    return terms[0]


def cp_sum_kernel(after, back, onward, *refs):
    got = refs[:-3]
    part, back_out, onward_out = refs[-3:]
    part[...] = tree_sum([ref[...].astype(F32) for ref in got]).astype(BF)
    back_out[...] = back[...]
    onward_out[...] = onward[...]


def z_sum_kernel(after, *refs):
    refs[-1][...] = tree_sum([ref[...].astype(F32) for ref in refs[:-1]])


def final_kernel(after, mine, theirs, weight_grad, conv_grad):
    width = weight_grad.shape[1]
    half = weight_grad.shape[0] // 2
    cut = width // 4
    core = lax.rem(lax.axis_index("dp"), 2)
    for side, grads in ((core, mine), (1 - core, theirs)):
        for at in range(0, half, 16):
            block = grads[:, at // 16 * width : (at // 16 + 1) * width]
            weight_grad[pl.ds(pl.multiple_of(side * half + at, 16), 16)] = block
        conv = grads[:, half // 16 * width :]
        for part in range(2):
            cols = pl.ds(pl.multiple_of((2 * side + part) * cut, cut), cut)
            conv_grad[:, cols] = conv[8 * part : 8 * part + KW]


def weight_stack_kernel(after, *refs):
    for k, ref in enumerate(refs[:-1]):
        refs[-1][k] = ref[...]


def own_columns_kernel(order, after, w, *refs):
    wx = refs[-1]
    shard, width = w.shape
    place = lax.axis_index("cp")
    core = lax.rem(lax.axis_index("dp"), 2)
    wx[pl.ds(pl.multiple_of(place * shard, shard), shard)] = w[:, half_cols(core, width)]
    for by, ref in zip(order, refs[:-1]):
        at = lax.bitwise_xor(place, by) * shard
        wx[pl.ds(pl.multiple_of(at, shard), shard)] = ref[...]


def conv_kernel(att, wx, stream, g, near, far, facts, other, conv, gx, mixed):
    rows, width = g.shape
    core = lax.rem(lax.axis_index("dp"), 2)
    base = lax.axis_index("cp") * rows
    length = facts[0:1, 0:1]
    cols = half_cols(core, width)
    fill_half(gx.at[0], core, g, near, far, base, length)
    put(gx.at[1], 0, other[2 * rows :].astype(F32))
    mixed[0] = masked(stream[:, cols], base, length) + nn(att[...], wx[...])
    mixed[1] = other[rows : 2 * rows].astype(F32) + nn(other[0:rows], wx[...])
    conv[KW:] = jnp.zeros((8 - KW, conv.shape[1]), F32)
    for chunk in range(gx.shape[1]):
        here = slice(chunk * LANE, (chunk + 1) * LANE)
        blocks = [mixed[0, :, here], mixed[1, :, here]]
        for tap in range(KW):
            first = 8 + HALF - tap
            conv[tap : tap + 1, here] = jnp.sum(
                blocks[0] * gx[0, chunk, first : first + rows]
                + blocks[1] * gx[1, chunk, first : first + rows],
                axis=0,
                keepdims=True,
            )


def backward_kernel(
    after, q, k, v, near, far, stream_grad, facts, w, passed, *refs
):
    got = refs[:-12]
    query_g, key_g, value_g, back, onward, token, kx, vx, kg, vg, ag, wx = refs[-12:]
    rows, feats = q.shape
    place = lax.axis_index("cp")
    core = lax.rem(lax.axis_index("dp"), 2)
    shard, width = w.shape
    wx[pl.ds(pl.multiple_of(place * shard, shard), shard)] = w[...]
    for by, ref in enumerate(got, 1):
        at = pl.ds(pl.multiple_of(lax.bitwise_xor(place, by) * shard, shard), shard)
        wx[at, half_cols(core, width)] = ref[...]
        wx[at, half_cols(1 - core, width)] = passed[by - 1]
    base = lax.axis_index("cp") * rows
    length = facts[0:1, 0:1]
    ag[...] = nt(stream_grad[...], wx[...]).astype(BF)
    fill_ext(kx, vx, k, v, near, far)
    kg[...] = jnp.zeros_like(kg)
    vg[...] = jnp.zeros_like(vg)
    for tile in range(rows // TILE):
        start = tile * TILE
        allowed = allowed_in(tile, base, length, facts[1:2, 0:1], facts[2:3, 0:1])
        span = slice(start, start + REACH)
        for group in range(feats // FEATS):
            cols = slice(group * FEATS, (group + 1) * FEATS)
            query_stack = stacked(q[start : start + TILE, cols], HSZ**-0.5)
            grad_stack = stacked(ag[start : start + TILE, cols], 1.0)
            probs = probabilities(kx[span, cols], query_stack, allowed)
            dprob = nt(vx[span, cols], grad_stack)
            inner = jnp.sum(probs * dprob, axis=0, keepdims=True)
            dscore = (probs * (dprob - inner)).astype(BF)
            query_g[start : start + TILE, cols] = (
                unstacked(tn(dscore, kx[span, cols])) * HSZ**-0.5
            ).astype(BF)
            kg[span, cols] += nn(dscore, query_stack)
            vg[span, cols] += nn(probs.astype(BF), grad_stack)
    key_g[...] = kg[BACK : BACK + rows]
    value_g[...] = vg[BACK : BACK + rows]
    for at, ext in ((0, kg), (1, vg)):
        back[at * BACK : (at + 1) * BACK] = ext[0:BACK].astype(BF)
    span = slice(BACK + rows, BACK + rows + BLK)
    onward[...] = jnp.concatenate([kg[span], vg[span]], 0).astype(BF)
    token[...] = jnp.zeros_like(token)


def join_kernel(key_g, value_g, last, first, key_out, value_out, token):
    rows = key_g.shape[0]
    for at, grad, out in ((0, key_g, key_out), (1, value_g, value_out)):
        before = first[...].astype(F32)[at * BLK : (at + 1) * BLK]
        zeros = jnp.zeros((AHEAD - BLK, before.shape[1]), F32)
        out[0:AHEAD] = (grad[0:AHEAD] + jnp.concatenate([before, zeros], 0)).astype(BF)
        out[AHEAD : rows - BACK] = grad[AHEAD : rows - BACK].astype(BF)
        out[rows - BACK :] = (
            grad[rows - BACK :] + last[at * BACK : (at + 1) * BACK].astype(F32)
        ).astype(BF)
    token[...] = jnp.zeros_like(token)


def body(
    queries, key_rows, value_rows, stream_in, out_grad, out_weight, conv_weight, lengths, offsets
):
    rows, feats = queries.shape[1:]
    width = stream_in.shape[2]
    cps, dps = lax.axis_size("cp"), lax.axis_size("dp")
    floors = dps // 2
    q, k, v, g, stream = queries[0], key_rows[0], value_rows[0], out_grad[0], stream_in[0]
    shard = out_weight.shape[0]
    half = shard // 2
    ext = rows + BACK + AHEAD
    upward = [(i, (i + 1) % cps) for i in range(cps)]
    downward = [(i, (i - 1) % cps) for i in range(cps)]

    def over_cp(arrays, order):
        got = [
            lax.ppermute(arrays[by - 1], "cp", [(i, i ^ by) for i in range(cps)])
            for by in order
        ]
        return [got[order.index(by)] for by in range(1, cps)]

    def over_z(array):
        got = [
            lax.ppermute(array, "dp", [(i, i ^ (2 * by)) for i in range(dps)])
            for by in range(floors - 1, 0, -1)
        ]
        return got[::-1]

    def over_core(array):
        return lax.ppermute(array, "dp", [(i, i ^ 1) for i in range(dps)])

    ahead, behind, w_half = packed(k, v, g, out_weight)
    near = lax.ppermute(ahead, "cp", upward)
    far = lax.ppermute(behind, "cp", downward)
    inner, facts = call(
        inner_conv_kernel,
        (shape((rows, width), BF), shape((8, 128), jnp.int32)),
        [VMEM] * 2 + [pl.BlockSpec(memory_space=pltpu.SMEM), ANY],
        (g, conv_weight, lengths, pltpu.with_memory_space_constraint(offsets, pltpu.HBM)),
        [
            pltpu.VMEM((width // LANE, rows + 16, LANE), F32),
            pltpu.SMEM((1, 2), jnp.int32),
            pltpu.SemaphoreType.DMA,
        ],
    )
    falling, rising = list(range(cps - 1, 0, -1)), list(range(1, cps))
    w_got = over_cp([w_half] * (cps - 1), falling)
    ext_scratch = [pltpu.VMEM((ext, feats), BF)] * 2
    att, conv_send = call(
        forward_kernel,
        (shape((rows, feats), BF), shape((3 * rows + 16, width // 2), BF)),
        [VMEM] * 8,
        (q, k, v, near, far, g, stream, facts),
        ext_scratch + [pltpu.VMEM((width // 2 // LANE, rows + 16, LANE), F32)],
        flops=2**32,
    )
    conv_got = over_core(conv_send)
    stream_grad, send, keep = call(
        weights_kernel,
        (
            shape((rows, width), BF),
            shape((cps, half, width), BF),
            shape((cps, half, width), F32),
        ),
        [VMEM] * 7,
        (att, near, far, g, conv_weight, inner, facts),
        [pltpu.VMEM((width // LANE, 64, LANE), F32), pltpu.VMEM((feats, rows), BF)],
    )
    core_got = over_core(send)
    w_order = W_ORDER if cps == 4 else tuple(range(1, cps))
    w_cols = call(
        functools.partial(own_columns_kernel, w_order),
        shape((feats, width // 2), BF),
        [ANY] + [VMEM] * cps,
        (send, out_weight, *ordered(w_got, w_order)),
        flops=2**34,
    )
    conv = call(
        conv_kernel,
        shape((8, width // 2), F32),
        [VMEM] * 8,
        (att, w_cols, stream, g, near, far, facts, conv_got),
        [
            pltpu.VMEM((2, width // 2 // LANE, rows + 16, LANE), F32),
            pltpu.VMEM((2, rows, width // 2), F32),
        ],
    )
    wide = half // 16 * width + width // 4
    own, *pieces = call(
        split_kernel,
        (shape((16, wide), F32),) + (shape((16, wide), BF),) * (cps - 1),
        [VMEM] * 3,
        (keep, core_got, conv),
    )
    cp_got = over_cp(pieces, rising)
    token = shape((8, 128), F32)
    passed = over_core(
        call(
            weight_stack_kernel,
            shape((cps - 1, shard, width // 2), BF),
            [ANY] + [VMEM] * (cps - 1),
            (own, *w_got),
        )
    )
    query_g, key_g, value_g, back, onward, bwd_done = call(
        backward_kernel,
        (
            shape((rows, feats), BF),
            shape((rows, feats), F32),
            shape((rows, feats), F32),
            shape((2 * BACK, feats), BF),
            shape((2 * BLK, feats), BF),
            token,
        ),
        [ANY] + [VMEM] * (8 + cps),
        (own, q, k, v, near, far, stream_grad, facts, out_weight, passed, *w_got),
        ext_scratch
        + [pltpu.VMEM((ext, feats), F32)] * 2
        + [pltpu.VMEM((rows, feats), BF), pltpu.VMEM((feats, width), BF)],
        moved=10 * 2**20,
    )
    part, back, onward = call(
        cp_sum_kernel,
        (shape((16, wide), BF), shape(back.shape, BF), shape(onward.shape, BF)),
        [VMEM] * (cps + 3),
        (bwd_done, back, onward, own, *ordered(cp_got, CP_ORDER)),
    )
    last = lax.ppermute(back, "cp", downward)
    first = lax.ppermute(onward, "cp", upward)
    key_grad, value_grad, join_done = call(
        join_kernel,
        (shape((rows, feats), BF),) * 2 + (token,),
        [VMEM] * 4,
        (key_g, value_g, last, first),
    )
    if floors != 4:
        core = lax.axis_index("dp") % 2
        blocks = [part[:, at * width : (at + 1) * width] for at in range(half // 16)]
        summed = jnp.concatenate(blocks, 0).astype(F32)
        weights = lax.dynamic_update_slice(
            jnp.zeros((shard, width), F32), summed, (core * half, 0)
        )
        taps = lax.dynamic_update_slice(
            jnp.zeros((8, width), F32), conv, (0, core * (width // 2))
        )
        weight_grad = lax.psum(weights, "dp")
        conv_grad = lax.psum(taps, ("cp", "dp"))[:KW]
    else:
        mine = call(
            z_sum_kernel,
            shape((16, wide), F32),
            [VMEM] * (floors + 1),
            (join_done, part, *ordered(over_z(part), Z_ORDER)),
        )
        weight_grad, conv_grad = call(
            final_kernel,
            (shape((shard, width), F32), shape((KW, width), F32)),
            [VMEM] * 3,
            (join_done, mine, over_core(mine)),
        )
    return (
        query_g[None],
        key_grad[None],
        value_grad[None],
        stream_grad[None],
        weight_grad,
        conv_grad,
    )


def solution(mesh):
    rows_spec = P("dp", "cp", None)
    return jax.shard_map(
        body,
        mesh=mesh,
        in_specs=(rows_spec,) * 5 + (P("cp", None), P(), P("dp"), P("dp", None)),
        out_specs=(rows_spec,) * 4 + (P("cp", None), P()),
        check_vma=False,
    )
```

```python
import functools

import jax
import jax.numpy as jnp
from jax import lax
from jax.experimental import pallas as pl
from jax.experimental.pallas import tpu as pltpu
from jax.sharding import PartitionSpec as P

HEADS = 8
HSZ = 64
BLK = 24
KW = 7
HALF = KW // 2
BACK = 2 * BLK
AHEAD = 32
EDGE = 16
TILE = 4 * BLK
REACH = 176
GROUP = 4
FEATS = GROUP * HSZ
LANES = GROUP * TILE
LANE = 128
NEG = -1e30
W_ORDER = (1, 2, 3)
CP_ORDER = (1, 2, 3)
Z_ORDER = (3, 1, 2)
BF = jnp.bfloat16
F32 = jnp.float32
VMEM = pl.BlockSpec(memory_space=pltpu.VMEM)
ANY = pl.BlockSpec(memory_space=pl.ANY)


def nt(a, b):
    return lax.dot_general(a, b, (((1,), (1,)), ((), ())), preferred_element_type=F32)


def nn(a, b):
    return lax.dot_general(a, b, (((1,), (0,)), ((), ())), preferred_element_type=F32)


def tn(a, b):
    return lax.dot_general(a, b, (((0,), (0,)), ((), ())), preferred_element_type=F32)


def call(kernel, outs, ins, args, scratch=(), flops=0, moved=0):
    return pl.pallas_call(
        kernel,
        out_shape=outs,
        in_specs=ins,
        out_specs=jax.tree.map(lambda _: VMEM, outs),
        scratch_shapes=scratch,
        compiler_params=pltpu.CompilerParams(vmem_limit_bytes=40 * 1024 * 1024),
        cost_estimate=pl.CostEstimate(flops=flops, bytes_accessed=moved, transcendentals=0),
    )(*args)


def shape(dims, kind):
    return jax.ShapeDtypeStruct(dims, kind)


def half_cols(side, width):
    return pl.ds(pl.multiple_of(side * (width // 2), width // 2), width // 2)


def pack_kernel(
    k, v, g, w, ahead, behind, w_half, edge, first, sems,
):
    rows = k.shape[0]
    feats = k.shape[1]
    core = lax.rem(lax.axis_index("dp"), 2)
    pairs = [
        (k.at[pl.ds(rows - BACK, BACK)], ahead.at[pl.ds(0, BACK)]),
        (v.at[pl.ds(rows - BACK, BACK)], ahead.at[pl.ds(BACK, BACK)]),
        (k.at[pl.ds(0, AHEAD)], first.at[0]),
        (v.at[pl.ds(0, AHEAD)], first.at[1]),
        (g.at[pl.ds(rows - EDGE, EDGE)], edge.at[0]),
        (g.at[pl.ds(0, EDGE)], edge.at[1]),
        (w.at[:, half_cols(core, w.shape[1])], w_half),
    ]
    copies = [pltpu.make_async_copy(a, b, sems.at[i]) for i, (a, b) in enumerate(pairs)]
    for copy in copies:
        copy.start()
    for copy in copies:
        copy.wait()
    behind[0 : 2 * BLK] = jnp.concatenate(
        [first[0].astype(F32)[:BLK], first[1].astype(F32)[:BLK]], 0
    ).astype(BF)
    for out, block in ((ahead, edge[0].astype(F32)[8:]), (behind, edge[1].astype(F32)[:8])):
        two = jnp.concatenate([block[:, :feats], block[:, feats:]], 0)
        out[out.shape[0] - EDGE :] = two.astype(BF)


def packed(*args):
    feats, width = args[0].shape[1], args[2].shape[1]
    outs = (
        pltpu.VMEM((2 * BACK + EDGE, feats), BF),
        pltpu.VMEM((2 * BLK + EDGE, feats), BF),
        pltpu.VMEM((args[3].shape[0], width // 2), BF),
    )
    return pl.pallas_call(
        pack_kernel,
        out_shape=outs,
        in_specs=[ANY] * 4,
        out_specs=(VMEM,) * 3,
        scratch_shapes=[
            pltpu.VMEM((2, EDGE, width), BF),
            pltpu.VMEM((2, AHEAD, feats), BF),
            pltpu.SemaphoreType.DMA((7,)),
        ],
        compiler_params=pltpu.CompilerParams(vmem_limit_bytes=40 * 1024 * 1024),
    )(*[pltpu.with_memory_space_constraint(x, pltpu.HBM) for x in args])


def head_of(dims):
    return lax.broadcasted_iota(jnp.int32, dims, 1) // HSZ


def stacked(tile, amount):
    head = head_of((1, FEATS))
    return jnp.concatenate(
        [tile * jnp.where(head == h, amount, 0.0).astype(BF) for h in range(GROUP)], 0
    )


def unstacked(product):
    head = head_of((TILE, FEATS))
    out = product[:TILE]
    for h in range(1, GROUP):
        out = jnp.where(head == h, product[h * TILE : (h + 1) * TILE], out)
    return out


def fill_ext(kx, vx, k, v, near, far):
    rows = k.shape[0]
    for at, ext, local in ((0, kx, k), (1, vx, v)):
        ext[0:BACK] = near[at * BACK : (at + 1) * BACK]
        ext[BACK : BACK + rows] = local[...]
        after = far[0 : 2 * BLK].astype(F32)[at * BLK : (at + 1) * BLK]
        zeros = jnp.zeros((AHEAD - BLK, after.shape[1]), F32)
        ext[BACK + rows :] = jnp.concatenate([after, zeros], 0).astype(BF)


def allowed_in(tile, base, length, back, ahead):
    lane = lax.broadcasted_iota(jnp.int32, (1, LANES), 1)
    within = lane
    for h in range(1, GROUP):
        within = within - jnp.where(lane >= h * TILE, TILE, 0)
    block = jnp.zeros_like(lane)
    for b in range(1, TILE // BLK):
        block = block + jnp.where(within >= b * BLK, 1, 0)
    origin = base + tile * TILE - BACK
    low = jnp.maximum((block + 2 - back) * BLK, -origin)
    high = jnp.minimum((block + 3 + ahead) * BLK, length - origin)
    row = lax.broadcasted_iota(jnp.int32, (REACH, LANES), 0)
    return (row >= low) & (row < high)


def probabilities(key_tile, query_stack, allowed):
    scores = jnp.where(allowed, nt(key_tile, query_stack), NEG)
    terms = jnp.exp(scores - jnp.max(scores, axis=0, keepdims=True))
    return terms * (1.0 / jnp.sum(terms, axis=0, keepdims=True))


def masked(block, start, length):
    frame = start + lax.broadcasted_iota(jnp.int32, block.shape, 0)
    return jnp.where((frame >= 0) & (frame < length), block.astype(F32), 0.0)


def put(gx, at, block):
    for chunk in range(gx.shape[0]):
        gx[chunk, at : at + block.shape[0]] = block[:, chunk * LANE : (chunk + 1) * LANE]


def rims(near, far, base, rows, length):
    before = near[2 * BACK :].astype(F32)
    after = far[2 * BLK :].astype(F32)
    return (
        masked(jnp.concatenate([before[:8], before[8:]], 1), base - 8, length),
        masked(jnp.concatenate([after[:8], after[8:]], 1), base + rows, length),
    )


def fill_half(gx, side, g, near, far, base, length):
    rows = g.shape[0]
    before = near[2 * BACK :].astype(F32)
    after = far[2 * BLK :].astype(F32)
    put(gx, 0, masked(jnp.where(side == 0, before[:8], before[8:]), base - 8, length))
    put(gx, 8, masked(g[:, half_cols(side, g.shape[1])], base, length))
    put(gx, 8 + rows, masked(jnp.where(side == 0, after[:8], after[8:]), base + rows, length))


def convolve(out, out_at, gx, gx_at, taps, start, count, length):
    frame = start + lax.broadcasted_iota(jnp.int32, (count, LANE), 0)
    for chunk in range(gx.shape[0]):
        cols = slice(chunk * LANE, (chunk + 1) * LANE)
        first = gx_at + HALF
        total = taps[0:1, cols] * gx[chunk, first : first + count]
        for tap in range(1, KW):
            first = gx_at + HALF - tap
            total = total + taps[tap : tap + 1, cols] * gx[chunk, first : first + count]
        out[out_at : out_at + count, cols] = jnp.where(frame < length, total, 0.0).astype(BF)


def inner_conv_kernel(g, taps, lengths, offsets, out, facts, gx, pair, sem):
    copy = pltpu.make_async_copy(offsets, pair, sem)
    copy.start()
    facts[0:1] = jnp.full((1, facts.shape[1]), lengths[0], jnp.int32)
    rows = g.shape[0]
    base = lax.axis_index("cp") * rows
    gx[:, 0:8] = jnp.zeros((gx.shape[0], 8, LANE), F32)
    gx[:, 8 + rows :] = jnp.zeros((gx.shape[0], 8, LANE), F32)
    length = facts[0:1, 0:1]
    put(gx, 8, masked(g[...], base, length))
    convolve(out, 0, gx, 8, taps, base, rows, length)
    copy.wait()
    for row in range(2):
        facts[row + 1 : row + 2] = jnp.full((1, facts.shape[1]), pair[0, row], jnp.int32)


def forward_kernel(q, k, v, near, far, g, stream, facts, att_out, send, kx, vx, half_gx):
    rows, feats = q.shape
    width = g.shape[1]
    core = lax.rem(lax.axis_index("dp"), 2)
    base = lax.axis_index("cp") * rows
    length = facts[0:1, 0:1]
    fill_ext(kx, vx, k, v, near, far)
    for tile in range(rows // TILE):
        start = tile * TILE
        allowed = allowed_in(tile, base, length, facts[1:2, 0:1], facts[2:3, 0:1])
        frame = base + start + lax.broadcasted_iota(jnp.int32, (TILE, FEATS), 0)
        for group in range(feats // FEATS):
            cols = slice(group * FEATS, (group + 1) * FEATS)
            query_stack = stacked(q[start : start + TILE, cols], HSZ**-0.5)
            probs = probabilities(kx[start : start + REACH, cols], query_stack, allowed)
            product = tn(probs.astype(BF), vx[start : start + REACH, cols])
            attended = jnp.where(frame < length, unstacked(product), 0.0).astype(BF)
            att_out[start : start + TILE, cols] = attended
            send[start : start + TILE, cols] = attended
    send[rows : 2 * rows] = masked(stream[:, half_cols(1 - core, width)], base, length).astype(BF)
    fill_half(half_gx, 1 - core, g, near, far, base, length)
    for chunk in range(half_gx.shape[0]):
        send[2 * rows :, chunk * LANE : (chunk + 1) * LANE] = half_gx[chunk].astype(BF)


def weights_kernel(att, near, far, g, taps, inner, facts, stream_grad, send, keep, gx, att_t):
    rows = att.shape[0]
    parts, half, width = keep.shape
    core = lax.rem(lax.axis_index("dp"), 2)
    base = lax.axis_index("cp") * rows
    length = facts[0:1, 0:1]
    turned = att[...].astype(F32).T.astype(BF)
    for part in range(parts):
        for side in range(2):
            at = jnp.where(core == side, parts * half, 0) + part * half
            att_t[pl.ds(pl.multiple_of(at, half), half)] = turned[
                (2 * part + side) * half : (2 * part + side + 1) * half
            ]
    before, after = rims(near, far, base, rows, length)
    put(gx, 0, before)
    put(gx, 8, masked(g[0:32].astype(F32)[:24], base, length))
    put(gx, 32, masked(g[rows - 32 :].astype(F32)[8:], base + rows - 24, length))
    put(gx, 56, after)
    stream_grad[EDGE : rows - EDGE] = inner[EDGE : rows - EDGE]
    convolve(stream_grad, 0, gx, 8, taps, base, EDGE, length)
    convolve(stream_grad, rows - EDGE, gx, 40, taps, base + rows - EDGE, EDGE, length)
    product = nn(att_t[...], stream_grad[...])
    for part in range(parts):
        send[part] = product[part * half : (part + 1) * half].astype(BF)
        keep[part] = product[(parts + part) * half : (parts + part + 1) * half]


def packed_grads(rows, conv):
    cut = conv.shape[1] // 2
    blocks = [rows[at : at + 16] for at in range(0, rows.shape[0], 16)]
    return jnp.concatenate(blocks + [jnp.concatenate([conv[:, :cut], conv[:, cut:]], 0)], 1)


def split_kernel(keep, got, conv, own, *pieces):
    place = lax.axis_index("cp")
    parts, half, width = keep.shape
    for by in range(parts):
        at = lax.bitwise_xor(place, by)
        block = packed_grads(keep[at] + got[at].astype(F32), conv[...].astype(BF).astype(F32))
        if by == 0:
            own[...] = block
        else:
            pieces[by - 1][...] = block.astype(BF)


def ordered(arrays, order):
    return [arrays[by - 1] for by in order] if len(arrays) == len(order) else arrays


def tree_sum(terms):
    while len(terms) > 1:
        terms = [a + b for a, b in zip(terms[::2], terms[1::2])]
    return terms[0]


def cp_sum_kernel(after, *refs):
    refs[-1][...] = tree_sum([ref[...].astype(F32) for ref in refs[:-1]]).astype(BF)


def z_sum_kernel(after, *refs):
    refs[-1][...] = tree_sum([ref[...].astype(F32) for ref in refs[:-1]])


def final_kernel(after, mine, theirs, weight_grad, conv_grad):
    width = weight_grad.shape[1]
    half = weight_grad.shape[0] // 2
    cut = width // 4
    core = lax.rem(lax.axis_index("dp"), 2)
    for side, grads in ((core, mine), (1 - core, theirs)):
        for at in range(0, half, 16):
            block = grads[:, at // 16 * width : (at // 16 + 1) * width]
            weight_grad[pl.ds(pl.multiple_of(side * half + at, 16), 16)] = block
        conv = grads[:, half // 16 * width :]
        for part in range(2):
            cols = pl.ds(pl.multiple_of((2 * side + part) * cut, cut), cut)
            conv_grad[:, cols] = conv[8 * part : 8 * part + KW]


def weight_stack_kernel(after, *refs):
    for k, ref in enumerate(refs[:-1]):
        refs[-1][k] = ref[...]


def own_columns_kernel(order, after, w, *refs):
    wx = refs[-1]
    shard, width = w.shape
    place = lax.axis_index("cp")
    core = lax.rem(lax.axis_index("dp"), 2)
    wx[pl.ds(pl.multiple_of(place * shard, shard), shard)] = w[:, half_cols(core, width)]
    for by, ref in zip(order, refs[:-1]):
        at = lax.bitwise_xor(place, by) * shard
        wx[pl.ds(pl.multiple_of(at, shard), shard)] = ref[...]


def conv_kernel(att, wx, stream, g, near, far, facts, other, conv, gx, mixed):
    rows, width = g.shape
    core = lax.rem(lax.axis_index("dp"), 2)
    base = lax.axis_index("cp") * rows
    length = facts[0:1, 0:1]
    cols = half_cols(core, width)
    fill_half(gx.at[0], core, g, near, far, base, length)
    put(gx.at[1], 0, other[2 * rows :].astype(F32))
    mixed[0] = masked(stream[:, cols], base, length) + nn(att[...], wx[...])
    mixed[1] = other[rows : 2 * rows].astype(F32) + nn(other[0:rows], wx[...])
    conv[KW:] = jnp.zeros((8 - KW, conv.shape[1]), F32)
    for chunk in range(gx.shape[1]):
        here = slice(chunk * LANE, (chunk + 1) * LANE)
        blocks = [mixed[0, :, here], mixed[1, :, here]]
        for tap in range(KW):
            first = 8 + HALF - tap
            conv[tap : tap + 1, here] = jnp.sum(
                blocks[0] * gx[0, chunk, first : first + rows]
                + blocks[1] * gx[1, chunk, first : first + rows],
                axis=0,
                keepdims=True,
            )


def backward_kernel(
    after, q, k, v, near, far, stream_grad, facts, w, passed, *refs
):
    got = refs[:-12]
    query_g, key_g, value_g, back, onward, token, kx, vx, kg, vg, ag, wx = refs[-12:]
    rows, feats = q.shape
    place = lax.axis_index("cp")
    core = lax.rem(lax.axis_index("dp"), 2)
    shard, width = w.shape
    wx[pl.ds(pl.multiple_of(place * shard, shard), shard)] = w[...]
    for by, ref in enumerate(got, 1):
        at = pl.ds(pl.multiple_of(lax.bitwise_xor(place, by) * shard, shard), shard)
        wx[at, half_cols(core, width)] = ref[...]
        wx[at, half_cols(1 - core, width)] = passed[by - 1]
    base = lax.axis_index("cp") * rows
    length = facts[0:1, 0:1]
    ag[...] = nt(stream_grad[...], wx[...]).astype(BF)
    fill_ext(kx, vx, k, v, near, far)
    kg[...] = jnp.zeros_like(kg)
    vg[...] = jnp.zeros_like(vg)
    for tile in range(rows // TILE):
        start = tile * TILE
        allowed = allowed_in(tile, base, length, facts[1:2, 0:1], facts[2:3, 0:1])
        span = slice(start, start + REACH)
        for group in range(feats // FEATS):
            cols = slice(group * FEATS, (group + 1) * FEATS)
            query_stack = stacked(q[start : start + TILE, cols], HSZ**-0.5)
            grad_stack = stacked(ag[start : start + TILE, cols], 1.0)
            probs = probabilities(kx[span, cols], query_stack, allowed)
            dprob = nt(vx[span, cols], grad_stack)
            inner = jnp.sum(probs * dprob, axis=0, keepdims=True)
            dscore = (probs * (dprob - inner)).astype(BF)
            query_g[start : start + TILE, cols] = (
                unstacked(tn(dscore, kx[span, cols])) * HSZ**-0.5
            ).astype(BF)
            kg[span, cols] += nn(dscore, query_stack)
            vg[span, cols] += nn(probs.astype(BF), grad_stack)
    key_g[...] = kg[BACK : BACK + rows]
    value_g[...] = vg[BACK : BACK + rows]
    for at, ext in ((0, kg), (1, vg)):
        back[at * BACK : (at + 1) * BACK] = ext[0:BACK].astype(BF)
    span = slice(BACK + rows, BACK + rows + BLK)
    onward[...] = jnp.concatenate([kg[span], vg[span]], 0).astype(BF)
    token[...] = jnp.zeros_like(token)


def join_kernel(key_g, value_g, last, first, key_out, value_out, token):
    rows = key_g.shape[0]
    for at, grad, out in ((0, key_g, key_out), (1, value_g, value_out)):
        before = first[...].astype(F32)[at * BLK : (at + 1) * BLK]
        zeros = jnp.zeros((AHEAD - BLK, before.shape[1]), F32)
        out[0:AHEAD] = (grad[0:AHEAD] + jnp.concatenate([before, zeros], 0)).astype(BF)
        out[AHEAD : rows - BACK] = grad[AHEAD : rows - BACK].astype(BF)
        out[rows - BACK :] = (
            grad[rows - BACK :] + last[at * BACK : (at + 1) * BACK].astype(F32)
        ).astype(BF)
    token[...] = jnp.zeros_like(token)


def body(
    queries, key_rows, value_rows, stream_in, out_grad, out_weight, conv_weight, lengths, offsets
):
    rows, feats = queries.shape[1:]
    width = stream_in.shape[2]
    cps, dps = lax.axis_size("cp"), lax.axis_size("dp")
    floors = dps // 2
    q, k, v, g, stream = queries[0], key_rows[0], value_rows[0], out_grad[0], stream_in[0]
    shard = out_weight.shape[0]
    half = shard // 2
    ext = rows + BACK + AHEAD
    upward = [(i, (i + 1) % cps) for i in range(cps)]
    downward = [(i, (i - 1) % cps) for i in range(cps)]

    def over_cp(arrays, order):
        got = [
            lax.ppermute(arrays[by - 1], "cp", [(i, i ^ by) for i in range(cps)])
            for by in order
        ]
        return [got[order.index(by)] for by in range(1, cps)]

    def over_z(array):
        got = [
            lax.ppermute(array, "dp", [(i, i ^ (2 * by)) for i in range(dps)])
            for by in range(floors - 1, 0, -1)
        ]
        return got[::-1]

    def over_core(array):
        return lax.ppermute(array, "dp", [(i, i ^ 1) for i in range(dps)])

    ahead, behind, w_half = packed(k, v, g, out_weight)
    near = lax.ppermute(ahead, "cp", upward)
    far = lax.ppermute(behind, "cp", downward)
    inner, facts = call(
        inner_conv_kernel,
        (shape((rows, width), BF), shape((8, 128), jnp.int32)),
        [VMEM] * 2 + [pl.BlockSpec(memory_space=pltpu.SMEM), ANY],
        (g, conv_weight, lengths, pltpu.with_memory_space_constraint(offsets, pltpu.HBM)),
        [
            pltpu.VMEM((width // LANE, rows + 16, LANE), F32),
            pltpu.SMEM((1, 2), jnp.int32),
            pltpu.SemaphoreType.DMA,
        ],
    )
    falling, rising = list(range(cps - 1, 0, -1)), list(range(1, cps))
    w_got = over_cp([w_half] * (cps - 1), falling)
    ext_scratch = [pltpu.VMEM((ext, feats), BF)] * 2
    att, conv_send = call(
        forward_kernel,
        (shape((rows, feats), BF), shape((3 * rows + 16, width // 2), BF)),
        [VMEM] * 8,
        (q, k, v, near, far, g, stream, facts),
        ext_scratch + [pltpu.VMEM((width // 2 // LANE, rows + 16, LANE), F32)],
        flops=2**32,
    )
    conv_got = over_core(conv_send)
    stream_grad, send, keep = call(
        weights_kernel,
        (
            shape((rows, width), BF),
            shape((cps, half, width), BF),
            shape((cps, half, width), F32),
        ),
        [VMEM] * 7,
        (att, near, far, g, conv_weight, inner, facts),
        [pltpu.VMEM((width // LANE, 64, LANE), F32), pltpu.VMEM((feats, rows), BF)],
    )
    core_got = over_core(send)
    w_order = W_ORDER if cps == 4 else tuple(range(1, cps))
    w_cols = call(
        functools.partial(own_columns_kernel, w_order),
        shape((feats, width // 2), BF),
        [ANY] + [VMEM] * cps,
        (send, out_weight, *ordered(w_got, w_order)),
        flops=2**34,
    )
    conv = call(
        conv_kernel,
        shape((8, width // 2), F32),
        [VMEM] * 8,
        (att, w_cols, stream, g, near, far, facts, conv_got),
        [
            pltpu.VMEM((2, width // 2 // LANE, rows + 16, LANE), F32),
            pltpu.VMEM((2, rows, width // 2), F32),
        ],
    )
    wide = half // 16 * width + width // 4
    own, *pieces = call(
        split_kernel,
        (shape((16, wide), F32),) + (shape((16, wide), BF),) * (cps - 1),
        [VMEM] * 3,
        (keep, core_got, conv),
    )
    cp_got = over_cp(pieces, rising)
    token = shape((8, 128), F32)
    passed = over_core(
        call(
            weight_stack_kernel,
            shape((cps - 1, shard, width // 2), BF),
            [ANY] + [VMEM] * (cps - 1),
            (own, *w_got),
        )
    )
    query_g, key_g, value_g, back, onward, bwd_done = call(
        backward_kernel,
        (
            shape((rows, feats), BF),
            shape((rows, feats), F32),
            shape((rows, feats), F32),
            shape((2 * BACK, feats), BF),
            shape((2 * BLK, feats), BF),
            token,
        ),
        [ANY] + [VMEM] * (8 + cps),
        (own, q, k, v, near, far, stream_grad, facts, out_weight, passed, *w_got),
        ext_scratch
        + [pltpu.VMEM((ext, feats), F32)] * 2
        + [pltpu.VMEM((rows, feats), BF), pltpu.VMEM((feats, width), BF)],
        moved=10 * 2**20,
    )
    part = call(
        cp_sum_kernel,
        shape((16, wide), BF),
        [VMEM] * (cps + 1),
        (bwd_done, own, *ordered(cp_got, CP_ORDER)),
    )
    last = lax.ppermute(back, "cp", downward)
    first = lax.ppermute(onward, "cp", upward)
    key_grad, value_grad, join_done = call(
        join_kernel,
        (shape((rows, feats), BF),) * 2 + (token,),
        [VMEM] * 4,
        (key_g, value_g, last, first),
    )
    if floors != 4:
        core = lax.axis_index("dp") % 2
        blocks = [part[:, at * width : (at + 1) * width] for at in range(half // 16)]
        summed = jnp.concatenate(blocks, 0).astype(F32)
        weights = lax.dynamic_update_slice(
            jnp.zeros((shard, width), F32), summed, (core * half, 0)
        )
        taps = lax.dynamic_update_slice(
            jnp.zeros((8, width), F32), conv, (0, core * (width // 2))
        )
        weight_grad = lax.psum(weights, "dp")
        conv_grad = lax.psum(taps, ("cp", "dp"))[:KW]
    else:
        mine = call(
            z_sum_kernel,
            shape((16, wide), F32),
            [VMEM] * (floors + 1),
            (join_done, part, *ordered(over_z(part), Z_ORDER)),
        )
        weight_grad, conv_grad = call(
            final_kernel,
            (shape((shard, width), F32), shape((KW, width), F32)),
            [VMEM] * 3,
            (join_done, mine, over_core(mine)),
        )
    return (
        query_g[None],
        key_grad[None],
        value_grad[None],
        stream_grad[None],
        weight_grad,
        conv_grad,
    )


def solution(mesh):
    rows_spec = P("dp", "cp", None)
    return jax.shard_map(
        body,
        mesh=mesh,
        in_specs=(rows_spec,) * 5 + (P("cp", None), P(), P("dp"), P("dp", None)),
        out_specs=(rows_spec,) * 4 + (P("cp", None), P()),
        check_vma=False,
    )
```

```python
import functools

import jax
import jax.numpy as jnp
from jax import lax
from jax.experimental import pallas as pl
from jax.experimental.pallas import tpu as pltpu
from jax.sharding import PartitionSpec as P

HEADS = 8
HSZ = 64
BLK = 24
KW = 7
HALF = KW // 2
BACK = 2 * BLK
AHEAD = 32
EDGE = 16
TILE = 4 * BLK
REACH = 176
GROUP = 4
FEATS = GROUP * HSZ
LANES = GROUP * TILE
LANE = 128
NEG = -1e30
W_ORDER = (1, 2, 3)
CP_ORDER = (1, 2, 3)
BF = jnp.bfloat16
F32 = jnp.float32
VMEM = pl.BlockSpec(memory_space=pltpu.VMEM)
ANY = pl.BlockSpec(memory_space=pl.ANY)


def nt(a, b):
    return lax.dot_general(a, b, (((1,), (1,)), ((), ())), preferred_element_type=F32)


def nn(a, b):
    return lax.dot_general(a, b, (((1,), (0,)), ((), ())), preferred_element_type=F32)


def tn(a, b):
    return lax.dot_general(a, b, (((0,), (0,)), ((), ())), preferred_element_type=F32)


def call(kernel, outs, ins, args, scratch=(), flops=0, moved=0):
    return pl.pallas_call(
        kernel,
        out_shape=outs,
        in_specs=ins,
        out_specs=jax.tree.map(lambda _: VMEM, outs),
        scratch_shapes=scratch,
        compiler_params=pltpu.CompilerParams(vmem_limit_bytes=40 * 1024 * 1024),
        cost_estimate=pl.CostEstimate(flops=flops, bytes_accessed=moved, transcendentals=0),
    )(*args)


def shape(dims, kind):
    return jax.ShapeDtypeStruct(dims, kind)


def half_cols(side, width):
    return pl.ds(pl.multiple_of(side * (width // 2), width // 2), width // 2)


def pack_kernel(
    k, v, g, w, ahead, behind, w_half, edge, first, sems,
):
    rows = k.shape[0]
    feats = k.shape[1]
    core = lax.rem(lax.axis_index("dp"), 2)
    pairs = [
        (k.at[pl.ds(rows - BACK, BACK)], ahead.at[pl.ds(0, BACK)]),
        (v.at[pl.ds(rows - BACK, BACK)], ahead.at[pl.ds(BACK, BACK)]),
        (k.at[pl.ds(0, AHEAD)], first.at[0]),
        (v.at[pl.ds(0, AHEAD)], first.at[1]),
        (g.at[pl.ds(rows - EDGE, EDGE)], edge.at[0]),
        (g.at[pl.ds(0, EDGE)], edge.at[1]),
        (w.at[:, half_cols(core, w.shape[1])], w_half),
    ]
    copies = [pltpu.make_async_copy(a, b, sems.at[i]) for i, (a, b) in enumerate(pairs)]
    for copy in copies:
        copy.start()
    for copy in copies:
        copy.wait()
    behind[0 : 2 * BLK] = jnp.concatenate(
        [first[0].astype(F32)[:BLK], first[1].astype(F32)[:BLK]], 0
    ).astype(BF)
    for out, block in ((ahead, edge[0].astype(F32)[8:]), (behind, edge[1].astype(F32)[:8])):
        two = jnp.concatenate([block[:, :feats], block[:, feats:]], 0)
        out[out.shape[0] - EDGE :] = two.astype(BF)


def packed(*args):
    feats, width = args[0].shape[1], args[2].shape[1]
    outs = (
        pltpu.VMEM((2 * BACK + EDGE, feats), BF),
        pltpu.VMEM((2 * BLK + EDGE, feats), BF),
        pltpu.VMEM((args[3].shape[0], width // 2), BF),
    )
    return pl.pallas_call(
        pack_kernel,
        out_shape=outs,
        in_specs=[ANY] * 4,
        out_specs=(VMEM,) * 3,
        scratch_shapes=[
            pltpu.VMEM((2, EDGE, width), BF),
            pltpu.VMEM((2, AHEAD, feats), BF),
            pltpu.SemaphoreType.DMA((7,)),
        ],
        compiler_params=pltpu.CompilerParams(vmem_limit_bytes=40 * 1024 * 1024),
    )(*[pltpu.with_memory_space_constraint(x, pltpu.HBM) for x in args])


def head_of(dims):
    return lax.broadcasted_iota(jnp.int32, dims, 1) // HSZ


def stacked(tile, amount):
    head = head_of((1, FEATS))
    return jnp.concatenate(
        [tile * jnp.where(head == h, amount, 0.0).astype(BF) for h in range(GROUP)], 0
    )


def unstacked(product):
    head = head_of((TILE, FEATS))
    out = product[:TILE]
    for h in range(1, GROUP):
        out = jnp.where(head == h, product[h * TILE : (h + 1) * TILE], out)
    return out


def fill_ext(kx, vx, k, v, near, far):
    rows = k.shape[0]
    for at, ext, local in ((0, kx, k), (1, vx, v)):
        ext[0:BACK] = near[at * BACK : (at + 1) * BACK]
        ext[BACK : BACK + rows] = local[...]
        after = far[0 : 2 * BLK].astype(F32)[at * BLK : (at + 1) * BLK]
        zeros = jnp.zeros((AHEAD - BLK, after.shape[1]), F32)
        ext[BACK + rows :] = jnp.concatenate([after, zeros], 0).astype(BF)


def allowed_in(tile, base, length, back, ahead):
    lane = lax.broadcasted_iota(jnp.int32, (1, LANES), 1)
    within = lane
    for h in range(1, GROUP):
        within = within - jnp.where(lane >= h * TILE, TILE, 0)
    block = jnp.zeros_like(lane)
    for b in range(1, TILE // BLK):
        block = block + jnp.where(within >= b * BLK, 1, 0)
    origin = base + tile * TILE - BACK
    low = jnp.maximum((block + 2 - back) * BLK, -origin)
    high = jnp.minimum((block + 3 + ahead) * BLK, length - origin)
    row = lax.broadcasted_iota(jnp.int32, (REACH, LANES), 0)
    return (row >= low) & (row < high)


def probabilities(key_tile, query_stack, allowed):
    scores = jnp.where(allowed, nt(key_tile, query_stack), NEG)
    terms = jnp.exp(scores - jnp.max(scores, axis=0, keepdims=True))
    return terms * (1.0 / jnp.sum(terms, axis=0, keepdims=True))


def masked(block, start, length):
    frame = start + lax.broadcasted_iota(jnp.int32, block.shape, 0)
    return jnp.where((frame >= 0) & (frame < length), block.astype(F32), 0.0)


def put(gx, at, block):
    for chunk in range(gx.shape[0]):
        gx[chunk, at : at + block.shape[0]] = block[:, chunk * LANE : (chunk + 1) * LANE]


def rims(near, far, base, rows, length):
    before = near[2 * BACK :].astype(F32)
    after = far[2 * BLK :].astype(F32)
    return (
        masked(jnp.concatenate([before[:8], before[8:]], 1), base - 8, length),
        masked(jnp.concatenate([after[:8], after[8:]], 1), base + rows, length),
    )


def fill_half(gx, side, g, near, far, base, length):
    rows = g.shape[0]
    before = near[2 * BACK :].astype(F32)
    after = far[2 * BLK :].astype(F32)
    put(gx, 0, masked(jnp.where(side == 0, before[:8], before[8:]), base - 8, length))
    put(gx, 8, masked(g[:, half_cols(side, g.shape[1])], base, length))
    put(gx, 8 + rows, masked(jnp.where(side == 0, after[:8], after[8:]), base + rows, length))


def convolve(out, out_at, gx, gx_at, taps, start, count, length):
    frame = start + lax.broadcasted_iota(jnp.int32, (count, LANE), 0)
    for chunk in range(gx.shape[0]):
        cols = slice(chunk * LANE, (chunk + 1) * LANE)
        first = gx_at + HALF
        total = taps[0:1, cols] * gx[chunk, first : first + count]
        for tap in range(1, KW):
            first = gx_at + HALF - tap
            total = total + taps[tap : tap + 1, cols] * gx[chunk, first : first + count]
        out[out_at : out_at + count, cols] = jnp.where(frame < length, total, 0.0).astype(BF)


def inner_conv_kernel(g, taps, lengths, offsets, out, facts, gx, pair, sem):
    copy = pltpu.make_async_copy(offsets, pair, sem)
    copy.start()
    facts[0:1] = jnp.full((1, facts.shape[1]), lengths[0], jnp.int32)
    rows = g.shape[0]
    base = lax.axis_index("cp") * rows
    gx[:, 0:8] = jnp.zeros((gx.shape[0], 8, LANE), F32)
    gx[:, 8 + rows :] = jnp.zeros((gx.shape[0], 8, LANE), F32)
    length = facts[0:1, 0:1]
    put(gx, 8, masked(g[...], base, length))
    convolve(out, 0, gx, 8, taps, base, rows, length)
    copy.wait()
    for row in range(2):
        facts[row + 1 : row + 2] = jnp.full((1, facts.shape[1]), pair[0, row], jnp.int32)


def forward_kernel(q, k, v, near, far, g, stream, facts, att_out, send, kx, vx, half_gx):
    rows, feats = q.shape
    width = g.shape[1]
    core = lax.rem(lax.axis_index("dp"), 2)
    base = lax.axis_index("cp") * rows
    length = facts[0:1, 0:1]
    fill_ext(kx, vx, k, v, near, far)
    for tile in range(rows // TILE):
        start = tile * TILE
        allowed = allowed_in(tile, base, length, facts[1:2, 0:1], facts[2:3, 0:1])
        frame = base + start + lax.broadcasted_iota(jnp.int32, (TILE, FEATS), 0)
        for group in range(feats // FEATS):
            cols = slice(group * FEATS, (group + 1) * FEATS)
            query_stack = stacked(q[start : start + TILE, cols], HSZ**-0.5)
            probs = probabilities(kx[start : start + REACH, cols], query_stack, allowed)
            product = tn(probs.astype(BF), vx[start : start + REACH, cols])
            attended = jnp.where(frame < length, unstacked(product), 0.0).astype(BF)
            att_out[start : start + TILE, cols] = attended
            send[start : start + TILE, cols] = attended
    send[rows : 2 * rows] = masked(stream[:, half_cols(1 - core, width)], base, length).astype(BF)
    fill_half(half_gx, 1 - core, g, near, far, base, length)
    for chunk in range(half_gx.shape[0]):
        send[2 * rows :, chunk * LANE : (chunk + 1) * LANE] = half_gx[chunk].astype(BF)


def weights_kernel(att, near, far, g, taps, inner, facts, stream_grad, send, keep, gx, att_t):
    rows = att.shape[0]
    parts, half, width = keep.shape
    core = lax.rem(lax.axis_index("dp"), 2)
    base = lax.axis_index("cp") * rows
    length = facts[0:1, 0:1]
    turned = att[...].astype(F32).T.astype(BF)
    for part in range(parts):
        for side in range(2):
            at = jnp.where(core == side, parts * half, 0) + part * half
            att_t[pl.ds(pl.multiple_of(at, half), half)] = turned[
                (2 * part + side) * half : (2 * part + side + 1) * half
            ]
    before, after = rims(near, far, base, rows, length)
    put(gx, 0, before)
    put(gx, 8, masked(g[0:32].astype(F32)[:24], base, length))
    put(gx, 32, masked(g[rows - 32 :].astype(F32)[8:], base + rows - 24, length))
    put(gx, 56, after)
    stream_grad[EDGE : rows - EDGE] = inner[EDGE : rows - EDGE]
    convolve(stream_grad, 0, gx, 8, taps, base, EDGE, length)
    convolve(stream_grad, rows - EDGE, gx, 40, taps, base + rows - EDGE, EDGE, length)
    product = nn(att_t[...], stream_grad[...])
    for part in range(parts):
        send[part] = product[part * half : (part + 1) * half].astype(BF)
        keep[part] = product[(parts + part) * half : (parts + part + 1) * half]


def packed_grads(rows, conv):
    cut = conv.shape[1] // 2
    blocks = [rows[at : at + 16] for at in range(0, rows.shape[0], 16)]
    return jnp.concatenate(blocks + [jnp.concatenate([conv[:, :cut], conv[:, cut:]], 0)], 1)


def split_kernel(keep, got, conv, own, *pieces):
    place = lax.axis_index("cp")
    parts, half, width = keep.shape
    for by in range(parts):
        at = lax.bitwise_xor(place, by)
        block = packed_grads(keep[at] + got[at].astype(F32), conv[...].astype(BF).astype(F32))
        if by == 0:
            own[...] = block
        else:
            pieces[by - 1][...] = block.astype(BF)


def ordered(arrays, order):
    return [arrays[by - 1] for by in order] if len(arrays) == len(order) else arrays


def tree_sum(terms):
    while len(terms) > 1:
        terms = [a + b for a, b in zip(terms[::2], terms[1::2])]
    return terms[0]


def cp_sum_kernel(after, back, onward, *refs):
    got = refs[:-3]
    part, back_out, onward_out = refs[-3:]
    part[...] = tree_sum([ref[...].astype(F32) for ref in got]).astype(BF)
    back_out[...] = back[...]
    onward_out[...] = onward[...]


def z_sum_kernel(after, *refs):
    refs[-1][...] = tree_sum([ref[...].astype(F32) for ref in refs[:-1]])


def final_kernel(after, mine, theirs, weight_grad, conv_grad):
    width = weight_grad.shape[1]
    half = weight_grad.shape[0] // 2
    cut = width // 4
    core = lax.rem(lax.axis_index("dp"), 2)
    for side, grads in ((core, mine), (1 - core, theirs)):
        for at in range(0, half, 16):
            block = grads[:, at // 16 * width : (at // 16 + 1) * width]
            weight_grad[pl.ds(pl.multiple_of(side * half + at, 16), 16)] = block
        conv = grads[:, half // 16 * width :]
        for part in range(2):
            cols = pl.ds(pl.multiple_of((2 * side + part) * cut, cut), cut)
            conv_grad[:, cols] = conv[8 * part : 8 * part + KW]


def weight_stack_kernel(after, *refs):
    for k, ref in enumerate(refs[:-1]):
        refs[-1][k] = ref[...]


def own_columns_kernel(order, after, w, *refs):
    wx = refs[-1]
    shard, width = w.shape
    place = lax.axis_index("cp")
    core = lax.rem(lax.axis_index("dp"), 2)
    wx[pl.ds(pl.multiple_of(place * shard, shard), shard)] = w[:, half_cols(core, width)]
    for by, ref in zip(order, refs[:-1]):
        at = lax.bitwise_xor(place, by) * shard
        wx[pl.ds(pl.multiple_of(at, shard), shard)] = ref[...]


def conv_kernel(att, wx, stream, g, near, far, facts, other, conv, gx, mixed):
    rows, width = g.shape
    core = lax.rem(lax.axis_index("dp"), 2)
    base = lax.axis_index("cp") * rows
    length = facts[0:1, 0:1]
    cols = half_cols(core, width)
    fill_half(gx.at[0], core, g, near, far, base, length)
    put(gx.at[1], 0, other[2 * rows :].astype(F32))
    mixed[0] = masked(stream[:, cols], base, length) + nn(att[...], wx[...])
    mixed[1] = other[rows : 2 * rows].astype(F32) + nn(other[0:rows], wx[...])
    conv[KW:] = jnp.zeros((8 - KW, conv.shape[1]), F32)
    for chunk in range(gx.shape[1]):
        here = slice(chunk * LANE, (chunk + 1) * LANE)
        blocks = [mixed[0, :, here], mixed[1, :, here]]
        for tap in range(KW):
            first = 8 + HALF - tap
            conv[tap : tap + 1, here] = jnp.sum(
                blocks[0] * gx[0, chunk, first : first + rows]
                + blocks[1] * gx[1, chunk, first : first + rows],
                axis=0,
                keepdims=True,
            )


def backward_kernel(
    after, q, k, v, near, far, stream_grad, facts, w, passed, *refs
):
    got = refs[:-12]
    query_g, key_g, value_g, back, onward, token, kx, vx, kg, vg, ag, wx = refs[-12:]
    rows, feats = q.shape
    place = lax.axis_index("cp")
    core = lax.rem(lax.axis_index("dp"), 2)
    shard, width = w.shape
    wx[pl.ds(pl.multiple_of(place * shard, shard), shard)] = w[...]
    for by, ref in enumerate(got, 1):
        at = pl.ds(pl.multiple_of(lax.bitwise_xor(place, by) * shard, shard), shard)
        wx[at, half_cols(core, width)] = ref[...]
        wx[at, half_cols(1 - core, width)] = passed[by - 1]
    base = lax.axis_index("cp") * rows
    length = facts[0:1, 0:1]
    ag[...] = nt(stream_grad[...], wx[...]).astype(BF)
    fill_ext(kx, vx, k, v, near, far)
    kg[...] = jnp.zeros_like(kg)
    vg[...] = jnp.zeros_like(vg)
    for tile in range(rows // TILE):
        start = tile * TILE
        allowed = allowed_in(tile, base, length, facts[1:2, 0:1], facts[2:3, 0:1])
        span = slice(start, start + REACH)
        for group in range(feats // FEATS):
            cols = slice(group * FEATS, (group + 1) * FEATS)
            query_stack = stacked(q[start : start + TILE, cols], HSZ**-0.5)
            grad_stack = stacked(ag[start : start + TILE, cols], 1.0)
            probs = probabilities(kx[span, cols], query_stack, allowed)
            dprob = nt(vx[span, cols], grad_stack)
            inner = jnp.sum(probs * dprob, axis=0, keepdims=True)
            dscore = (probs * (dprob - inner)).astype(BF)
            query_g[start : start + TILE, cols] = (
                unstacked(tn(dscore, kx[span, cols])) * HSZ**-0.5
            ).astype(BF)
            kg[span, cols] += nn(dscore, query_stack)
            vg[span, cols] += nn(probs.astype(BF), grad_stack)
    key_g[...] = kg[BACK : BACK + rows]
    value_g[...] = vg[BACK : BACK + rows]
    for at, ext in ((0, kg), (1, vg)):
        back[at * BACK : (at + 1) * BACK] = ext[0:BACK].astype(BF)
    span = slice(BACK + rows, BACK + rows + BLK)
    onward[...] = jnp.concatenate([kg[span], vg[span]], 0).astype(BF)
    token[...] = jnp.zeros_like(token)


def join_kernel(key_g, value_g, last, first, key_out, value_out, token):
    rows = key_g.shape[0]
    for at, grad, out in ((0, key_g, key_out), (1, value_g, value_out)):
        before = first[...].astype(F32)[at * BLK : (at + 1) * BLK]
        zeros = jnp.zeros((AHEAD - BLK, before.shape[1]), F32)
        out[0:AHEAD] = (grad[0:AHEAD] + jnp.concatenate([before, zeros], 0)).astype(BF)
        out[AHEAD : rows - BACK] = grad[AHEAD : rows - BACK].astype(BF)
        out[rows - BACK :] = (
            grad[rows - BACK :] + last[at * BACK : (at + 1) * BACK].astype(F32)
        ).astype(BF)
    token[...] = jnp.zeros_like(token)


def body(
    queries, key_rows, value_rows, stream_in, out_grad, out_weight, conv_weight, lengths, offsets
):
    rows, feats = queries.shape[1:]
    width = stream_in.shape[2]
    cps, dps = lax.axis_size("cp"), lax.axis_size("dp")
    floors = dps // 2
    q, k, v, g, stream = queries[0], key_rows[0], value_rows[0], out_grad[0], stream_in[0]
    shard = out_weight.shape[0]
    half = shard // 2
    ext = rows + BACK + AHEAD
    upward = [(i, (i + 1) % cps) for i in range(cps)]
    downward = [(i, (i - 1) % cps) for i in range(cps)]

    def over_cp(arrays, order):
        got = [
            lax.ppermute(arrays[by - 1], "cp", [(i, i ^ by) for i in range(cps)])
            for by in order
        ]
        return [got[order.index(by)] for by in range(1, cps)]

    def over_z(array, by):
        return lax.ppermute(array, "dp", [(i, i ^ (2 * by)) for i in range(dps)])

    def over_core(array):
        return lax.ppermute(array, "dp", [(i, i ^ 1) for i in range(dps)])

    ahead, behind, w_half = packed(k, v, g, out_weight)
    near = lax.ppermute(ahead, "cp", upward)
    far = lax.ppermute(behind, "cp", downward)
    inner, facts = call(
        inner_conv_kernel,
        (shape((rows, width), BF), shape((8, 128), jnp.int32)),
        [VMEM] * 2 + [pl.BlockSpec(memory_space=pltpu.SMEM), ANY],
        (g, conv_weight, lengths, pltpu.with_memory_space_constraint(offsets, pltpu.HBM)),
        [
            pltpu.VMEM((width // LANE, rows + 16, LANE), F32),
            pltpu.SMEM((1, 2), jnp.int32),
            pltpu.SemaphoreType.DMA,
        ],
    )
    falling, rising = list(range(cps - 1, 0, -1)), list(range(1, cps))
    w_got = over_cp([w_half] * (cps - 1), falling)
    ext_scratch = [pltpu.VMEM((ext, feats), BF)] * 2
    att, conv_send = call(
        forward_kernel,
        (shape((rows, feats), BF), shape((3 * rows + 16, width // 2), BF)),
        [VMEM] * 8,
        (q, k, v, near, far, g, stream, facts),
        ext_scratch + [pltpu.VMEM((width // 2 // LANE, rows + 16, LANE), F32)],
        flops=2**32,
    )
    conv_got = over_core(conv_send)
    stream_grad, send, keep = call(
        weights_kernel,
        (
            shape((rows, width), BF),
            shape((cps, half, width), BF),
            shape((cps, half, width), F32),
        ),
        [VMEM] * 7,
        (att, near, far, g, conv_weight, inner, facts),
        [pltpu.VMEM((width // LANE, 64, LANE), F32), pltpu.VMEM((feats, rows), BF)],
    )
    core_got = over_core(send)
    w_order = W_ORDER if cps == 4 else tuple(range(1, cps))
    w_cols = call(
        functools.partial(own_columns_kernel, w_order),
        shape((feats, width // 2), BF),
        [ANY] + [VMEM] * cps,
        (send, out_weight, *ordered(w_got, w_order)),
        flops=2**34,
    )
    conv = call(
        conv_kernel,
        shape((8, width // 2), F32),
        [VMEM] * 8,
        (att, w_cols, stream, g, near, far, facts, conv_got),
        [
            pltpu.VMEM((2, width // 2 // LANE, rows + 16, LANE), F32),
            pltpu.VMEM((2, rows, width // 2), F32),
        ],
    )
    wide = half // 16 * width + width // 4
    own, *pieces = call(
        split_kernel,
        (shape((16, wide), F32),) + (shape((16, wide), BF),) * (cps - 1),
        [VMEM] * 3,
        (keep, core_got, conv),
    )
    cp_got = over_cp(pieces, rising)
    token = shape((8, 128), F32)
    passed = over_core(
        call(
            weight_stack_kernel,
            shape((cps - 1, shard, width // 2), BF),
            [ANY] + [VMEM] * (cps - 1),
            (own, *w_got),
        )
    )
    query_g, key_g, value_g, back, onward, bwd_done = call(
        backward_kernel,
        (
            shape((rows, feats), BF),
            shape((rows, feats), F32),
            shape((rows, feats), F32),
            shape((2 * BACK, feats), BF),
            shape((2 * BLK, feats), BF),
            token,
        ),
        [ANY] + [VMEM] * (8 + cps),
        (own, q, k, v, near, far, stream_grad, facts, out_weight, passed, *w_got),
        ext_scratch
        + [pltpu.VMEM((ext, feats), F32)] * 2
        + [pltpu.VMEM((rows, feats), BF), pltpu.VMEM((feats, width), BF)],
        moved=10 * 2**20,
    )
    part, back, onward = call(
        cp_sum_kernel,
        (shape((16, wide), BF), shape(back.shape, BF), shape(onward.shape, BF)),
        [VMEM] * (cps + 3),
        (bwd_done, back, onward, own, *ordered(cp_got, CP_ORDER)),
    )
    last = lax.ppermute(back, "cp", downward)
    first = lax.ppermute(onward, "cp", upward)
    key_grad, value_grad, join_done = call(
        join_kernel,
        (shape((rows, feats), BF),) * 2 + (token,),
        [VMEM] * 4,
        (key_g, value_g, last, first),
        flops=2**30,
    )
    if floors != 4:
        core = lax.axis_index("dp") % 2
        blocks = [part[:, at * width : (at + 1) * width] for at in range(half // 16)]
        summed = jnp.concatenate(blocks, 0).astype(F32)
        weights = lax.dynamic_update_slice(
            jnp.zeros((shard, width), F32), summed, (core * half, 0)
        )
        taps = lax.dynamic_update_slice(
            jnp.zeros((8, width), F32), conv, (0, core * (width // 2))
        )
        weight_grad = lax.psum(weights, "dp")
        conv_grad = lax.psum(taps, ("cp", "dp"))[:KW]
    else:
        across = over_z(part, 2)
        beside = over_z(part, 1)
        mine = call(
            z_sum_kernel,
            shape((16, wide), F32),
            [VMEM] * (floors + 1),
            (join_done, part, beside, across, over_z(across, 1)),
        )
        weight_grad, conv_grad = call(
            final_kernel,
            (shape((shard, width), F32), shape((KW, width), F32)),
            [VMEM] * 3,
            (join_done, mine, over_core(mine)),
        )
    return (
        query_g[None],
        key_grad[None],
        value_grad[None],
        stream_grad[None],
        weight_grad,
        conv_grad,
    )


def solution(mesh):
    rows_spec = P("dp", "cp", None)
    return jax.shard_map(
        body,
        mesh=mesh,
        in_specs=(rows_spec,) * 5 + (P("cp", None), P(), P("dp"), P("dp", None)),
        out_specs=(rows_spec,) * 4 + (P("cp", None), P()),
        check_vma=False,
    )
```
